512 devices in a mesh: lat: 16 (over y_hi, z), lon: 32 (over y_lo, x, core).
Axes of the slice: x: 4, y: 8 (y_hi: 2, y_lo: 4; y = y_hi * 4 + y_lo), z: 8, core: 2. Of those that a mesh axis runs over, the one named last changes fastest.
Arguments:
- state: bfloat16 [1, 512, 2048, 128], P(None, 'lat', 'lon'), may hold values from -6 to 6
- obs_members: bfloat16 [16, 32, 512, 128], P('lat', 'lon'), may hold values from -6 to 6
- obs_values: float32 [16, 32, 512], P('lat', 'lon'), may hold values from -6 to 6
- obs_precision: float32 [16, 32, 512], P('lat', 'lon'), may hold values from 0.5 to 500
- obs_cells: int32 [16, 32, 512], P('lat', 'lon'), may hold values from 0 to 2047
- obs_counts: int32 [16, 32], P('lat', 'lon'), may hold values from 85 to 512, as said below
Outputs:
- analysis: bfloat16 [1, 512, 2048, 128], P(None, 'lat', 'lon')
The draws below stay inside these ranges and needn't reach their ends.
Inputs may be any that keep to these rules, and one draw needn't show every extreme that they name: `obs_counts`: exactly one tile uses all 512 slots; every other tile uses between 85 and 256 slots, and some other tile uses exactly 256.
All inputs are finite; a program needn't handle non-finite values.
Results may differ from the reference program's by a relative error of at most 0.0087.
Values may be sent and summed in bfloat16 or wider, within the bound.
No kernel may reach another device: no remote copies, remote signals or barrier semaphores. Data moves between devices by JAX's collectives and lax.ppermute only.
A program may use at most 64 MiB of HBM per device.

```python
import math
import jax
import jax.numpy as jnp
from jax import lax

MEMBERS = 128
LEVELS = 1
TILE_LAT = 32
TILE_LON = 64
CAP = 512
PATCH = 16
NS_STEPS = 12
RAD = 24
TILES_LAT = 16
TILES_LON = 32
NLAT = 512
NLON = 2048


def draw_obs_counts(key, part):
    key = jax.random.fold_in(key, 7)
    first_key, second_key, third_key = jax.random.split(key, 3)
    total = TILES_LAT * TILES_LON
    counts = jax.random.randint(first_key, (total,), CAP // 6, CAP // 2 + 1, dtype=jnp.int32)
    chosen = jax.random.randint(second_key, (), 0, total, dtype=jnp.int32)
    second = (chosen + 1 + jax.random.randint(third_key, (), 0, total - 1, dtype=jnp.int32)) % total
    tile_ids = jnp.arange(total, dtype=jnp.int32)
    counts = jnp.where(tile_ids == second, CAP // 2, counts)
    counts = jnp.where(tile_ids == chosen, CAP, counts)
    return counts.reshape(TILES_LAT, TILES_LON).astype(jnp.int32)


def set_ends(drawn, rng, smallest, high):
    longest = drawn.shape.index(max(drawn.shape))
    spots = []
    for shift in (0, 1):
        where = [jax.random.randint(jax.random.fold_in(rng, axis), (), 0, length) for axis, length in enumerate(drawn.shape)]
        where[longest] = (where[longest] + shift) % drawn.shape[longest]
        spots.append(tuple(where))
    return drawn.at[spots[0]].set(smallest).at[spots[1]].set(high)


def level_of(stream_key, dims, cuts, smallest, high):
    factor_of, own = 1.0, jax.random.fold_in(stream_key, 6)
    for position, shards_of in cuts:
        steps = jnp.exp(jax.random.uniform(jax.random.fold_in(own, position), (shards_of,), jnp.float32, smallest / len(cuts), high / len(cuts)))
        factor_of = factor_of * jnp.repeat(steps, dims[position] // shards_of).reshape([-1 if axis == position else 1 for axis in range(len(dims))])
    return factor_of


def normal_values(key, dims, deviation, limit, shards=(), kind=jnp.bfloat16):
    factor_of = level_of(key, dims, shards, -0.22, 0.18) if shards else 1.0
    entries = jax.random.normal(key, dims, jnp.float32) * deviation * factor_of
    return jnp.minimum(jnp.maximum(entries, -limit), limit).astype(kind)


def setup_inputs(seed: int = 0) -> dict:
    keys = jax.random.split(jax.random.key(seed), 7)
    return {
        "state": normal_values(keys[0], (LEVELS, NLAT, NLON, MEMBERS), 1.0, 6.0, ((1, 16), (2, 32))),
        "obs_members": normal_values(keys[1], (TILES_LAT, TILES_LON, CAP, MEMBERS), 1.0, 6.0, ((0, 16), (1, 32))),
        "obs_values": normal_values(keys[2], (TILES_LAT, TILES_LON, CAP), 1.0, 6.0, ((0, 16), (1, 32)), jnp.float32),
        "obs_precision": jnp.clip(jnp.exp(math.log(500.0) - 6.9077553 * jax.random.uniform(keys[3], (TILES_LAT, TILES_LON, CAP), jnp.float32) ** level_of(keys[3], (TILES_LAT, TILES_LON, CAP), ((0, 16), (1, 32)), -0.2, 0.2)), 0.5, 500.0),
        "obs_cells": set_ends(jax.random.randint(keys[4], (TILES_LAT, TILES_LON, CAP), 0, TILE_LAT * TILE_LON), jax.random.fold_in(keys[4], 1), 0, (TILE_LAT * TILE_LON) - 1).astype(jnp.int32),
        "obs_counts": draw_obs_counts(jax.random.fold_in(keys[6], 71), 0),
    }


def local_solve(members_near, scalars_near, tile_state, lat_here, lat_total):
    ensemble = members_near.shape[-1]
    levels, tile_rows, tile_cols, _ = tile_state.shape
    offsets = jnp.arange(3, dtype=jnp.int32) - 1
    lat_ok = ((lat_here + offsets >= 0) & (lat_here + offsets < lat_total)).astype(jnp.float32)
    values = scalars_near[:, :, 0, :].reshape(-1)
    weight = (scalars_near[:, :, 1, :] * lat_ok[:, None, None]).reshape(-1)
    obs_cells = scalars_near[:, :, 2, :].astype(jnp.int32)
    obs_rows = offsets[:, None, None] * tile_rows + obs_cells // tile_cols
    obs_cols = offsets[None, :, None] * tile_cols + obs_cells % tile_cols
    rows_twice = (2 * obs_rows + 1).reshape(-1)
    cols_twice = (2 * obs_cols + 1).reshape(-1)
    flattened = members_near.reshape(-1, ensemble)
    obs_mean = lax.optimization_barrier(jnp.sum(flattened, axis=1, dtype=jnp.float32)) / ensemble
    spread = (flattened.astype(jnp.float32) - obs_mean[:, None]).astype(jnp.bfloat16)
    innovation = values - obs_mean
    patch_cols = tile_cols // PATCH

    def patch_terms(patch_index):
        patch_row = patch_index // patch_cols
        patch_col = patch_index % patch_cols
        row_gap = rows_twice - (2 * patch_row * PATCH + PATCH)
        col_gap = cols_twice - (2 * patch_col * PATCH + PATCH)
        distance = row_gap * row_gap + col_gap * col_gap
        tapering = jnp.where(distance < 4 * RAD * RAD, jnp.exp(-distance.astype(jnp.float32) / (2.0 * RAD * RAD)), 0.0)
        local_weight = weight * tapering
        weighted = (local_weight[:, None] * spread.astype(jnp.float32)).astype(jnp.bfloat16)
        gram_part = lax.dot_general(weighted, spread, (((0,), (0,)), ((), ())), preferred_element_type=jnp.float32)
        pull_term = jnp.dot(innovation, weighted.astype(jnp.float32), precision=lax.Precision.HIGHEST)
        return (gram_part, pull_term)
    patches = tile_rows // PATCH * patch_cols
    grams, pulls = lax.map(patch_terms, jnp.arange(patches, dtype=jnp.int32))
    identity = jnp.eye(ensemble, dtype=jnp.float32)
    system = grams + (ensemble - 1.0) * identity
    trace_sum = jnp.trace(system, axis1=1, axis2=2)
    iterate = system / trace_sum[:, None, None]
    inverse_root = jnp.broadcast_to(identity, system.shape)
    for sweep_index in range(NS_STEPS):
        factor = 1.5 * identity - 0.5 * jnp.matmul(inverse_root, iterate, precision=lax.Precision.HIGHEST)
        iterate = jnp.matmul(iterate, factor, precision=lax.Precision.HIGHEST)
        inverse_root = jnp.matmul(factor, inverse_root, precision=lax.Precision.HIGHEST)
    spread_scale = jnp.sqrt((ensemble - 1.0) / trace_sum)
    inner = jnp.matmul(inverse_root, pulls[:, :, None], precision=lax.Precision.HIGHEST)
    mean_weights = jnp.matmul(inverse_root, inner, precision=lax.Precision.HIGHEST)[:, :, 0] / trace_sum[:, None]
    transform = (inverse_root * spread_scale[:, None, None] + mean_weights[:, :, None]).astype(jnp.bfloat16)
    state_mean = lax.optimization_barrier(jnp.sum(tile_state, axis=-1, dtype=jnp.float32)) / ensemble
    perturbation = (tile_state.astype(jnp.float32) - state_mean[..., None]).astype(jnp.bfloat16)
    blocks = perturbation.reshape(levels, tile_rows // PATCH, PATCH, patch_cols, PATCH, ensemble)
    matrices = transform.reshape(tile_rows // PATCH, patch_cols, ensemble, ensemble)
    updated = jnp.einsum('lapbqk,abkj->lapbqj', blocks.astype(jnp.float32), matrices.astype(jnp.float32))
    return (updated.reshape(levels, tile_rows, tile_cols, ensemble) + state_mean[..., None]).astype(jnp.bfloat16)

def surround(array):
    widths = ((1, 1),) + ((0, 0),) * (array.ndim - 1)
    padded = jnp.pad(array, widths)
    return jnp.concatenate([padded[:, -1:], padded, padded[:, :1]], axis=1)

def reference(state, obs_members, obs_values, obs_precision, obs_cells, obs_counts):
    slot_index = jnp.arange(CAP, dtype=jnp.int32)
    valid = (slot_index[None, None, :] < obs_counts[:, :, None]).astype(jnp.float32)
    scalars = jnp.stack([obs_values, obs_precision * valid, obs_cells.astype(jnp.float32)], axis=2)
    members_pad = surround(obs_members)
    scalars_pad = surround(scalars)
    zero = jnp.zeros((), jnp.int32)

    def one_tile(tile_index):
        lat_here = (tile_index // TILES_LON).astype(jnp.int32)
        lon_here = (tile_index % TILES_LON).astype(jnp.int32)
        members_near = lax.dynamic_slice(members_pad, (lat_here, lon_here, zero, zero), (3, 3, CAP, MEMBERS))
        scalars_near = lax.dynamic_slice(scalars_pad, (lat_here, lon_here, zero, zero), (3, 3, 3, CAP))
        tile_state = lax.dynamic_slice(state, (zero, lat_here * TILE_LAT, lon_here * TILE_LON, zero), (LEVELS, TILE_LAT, TILE_LON, MEMBERS))
        return local_solve(members_near, scalars_near, tile_state, lat_here, TILES_LAT)
    tiles = lax.map(one_tile, jnp.arange(TILES_LAT * TILES_LON, dtype=jnp.int32))
    tiles = tiles.reshape(TILES_LAT, TILES_LON, LEVELS, TILE_LAT, TILE_LON, MEMBERS)
    return tiles.transpose(2, 0, 3, 1, 4, 5).reshape(LEVELS, NLAT, NLON, MEMBERS)
```

```python
import functools

import jax
import jax.numpy as jnp
from jax import lax
from jax.experimental import pallas as pl
from jax.experimental.pallas import tpu as pltpu
from jax.sharding import PartitionSpec as P

PATCH = 16
NS_STEPS = 12
RAD = 24
EXTRA = 16
WEIGHT, ROW, COL = 2, 5, 6
F32, BF16 = jnp.float32, jnp.bfloat16


def halves(x):
    high = x.astype(BF16)
    return high, (x - high.astype(F32)).astype(BF16)


def thirds(x):
    high = x.astype(BF16)
    return high, *halves(x - high.astype(F32))


def side_by_side(x):
    return jnp.concatenate(halves(x), axis=1)


def pack_kernel(count_ref, members_ref, values_ref, precision_ref, cells_ref, out_ref, *, tile_cols):
    capacity, ensemble = members_ref.shape
    members = members_ref[...].T.astype(F32)
    mean = jnp.sum(members, axis=0, keepdims=True) * (1.0 / ensemble)
    out_ref[:ensemble, :] = (members - mean).astype(BF16)
    slot = lax.broadcasted_iota(jnp.int32, (1, capacity), 1)
    weight = jnp.where(slot < count_ref[0, 0], precision_ref[...], 0.0)
    cells = cells_ref[...]
    rows = [
        *halves(values_ref[...] - mean),
        *thirds(weight),
        (cells // tile_cols).astype(BF16),
        (cells % tile_cols).astype(BF16),
    ]
    index = lax.broadcasted_iota(jnp.int32, (EXTRA, capacity), 0)
    extra = jnp.zeros((EXTRA, capacity), F32)
    for at, row in enumerate(rows):
        extra = jnp.where(index == at, row.astype(F32), extra)
    out_ref[ensemble:, :] = extra.astype(BF16)


def locals_of(scalars, row_shift, col_shift, centres):
    high, middle, low = (scalars[WEIGHT + at : WEIGHT + at + 1] for at in range(3))
    weight = high + (middle + low)
    rows_twice = 2.0 * (scalars[ROW : ROW + 1] + row_shift) + 1.0
    cols_twice = 2.0 * (scalars[COL : COL + 1] + col_shift) + 1.0
    count = len(centres)
    index = lax.broadcasted_iota(jnp.int32, (8, 1), 0)
    row_centre = jnp.zeros((8, 1), F32)
    col_centre = jnp.zeros((8, 1), F32)
    for at, (row, col) in enumerate(centres):
        row_centre = jnp.where(index == at, row, row_centre)
        col_centre = jnp.where(index == at, col, col_centre)
    row_gap = rows_twice - row_centre
    col_gap = cols_twice - col_centre
    distance = row_gap * row_gap + col_gap * col_gap
    taper = jnp.where(distance < 4.0 * RAD * RAD, jnp.exp(-distance / (2.0 * RAD * RAD)), 0.0)
    local = weight * taper
    return [local[at : at + 1] for at in range(count)]


def add_grams(gram_ref, payload, shifts, patches, centres, ensemble):
    scalars = payload[ensemble:].astype(F32)
    spread = payload[:ensemble].astype(F32)
    local = locals_of(scalars, *shifts, [centres[p] for p in patches])
    weighted = jnp.concatenate([(row * spread).astype(BF16) for row in local], axis=0)
    part = lax.dot_general(weighted, payload, (((1,), (1,)), ((), ())), preferred_element_type=F32)
    for at, p in enumerate(patches):
        gram_ref[p] += part[at * ensemble : (at + 1) * ensemble]


def double_dot(left, right):
    width = right.shape[1] // 2
    both = jnp.dot(left, jnp.concatenate([right, right], axis=0), preferred_element_type=F32)
    return both[:, :width] + both[:, width:]


def solve(gram_ref, half_ref, z_ref, transform_ref, patches, ensemble):
    row = lax.broadcasted_iota(jnp.int32, (ensemble, ensemble), 0)
    col = lax.broadcasted_iota(jnp.int32, (ensemble, ensemble), 1)
    diagonal = row == col
    traces = []
    for p in range(patches):
        system = gram_ref[p, :, :ensemble] + jnp.where(diagonal, ensemble - 1.0, 0.0)
        on = jnp.where(diagonal, system, 0.0)
        trace = jnp.sum(jnp.sum(on, axis=0, keepdims=True), axis=1, keepdims=True)
        traces.append(trace)
        half = system * (-0.5 / trace)
        half_ref[p] = half
        z_ref[p] = jnp.where(diagonal, 1.5, 0.0) + half

    def times(matrix, column):
        across = jnp.sum(jnp.where(diagonal, column, 0.0), axis=0, keepdims=True)
        return jnp.sum(matrix * across, axis=1, keepdims=True)

    def advance_half(p, half, right):
        middle = 1.5 * half + double_dot(right, right)
        half_ref[p] = 1.5 * middle + double_dot(side_by_side(middle), right)

    for p in range(patches):
        half = half_ref[p]
        advance_half(p, half, side_by_side(half))

    def step(_, carry):
        for p in range(patches):
            half, z = half_ref[p], z_ref[p]
            right = side_by_side(half)
            left = jnp.concatenate([right, side_by_side(z)], axis=0)
            both = double_dot(left, right)
            middle = 1.5 * half + both[:ensemble]
            z_ref[p] = 1.5 * z + both[ensemble:]
            half_ref[p] = 1.5 * middle + double_dot(side_by_side(middle), right)
        return carry

    lax.fori_loop(0, NS_STEPS - 2, step, 0)
    for p in range(patches):
        half, z = half_ref[p], z_ref[p]
        z = 1.5 * z + double_dot(side_by_side(z), side_by_side(half))
        pull = gram_ref[p, :, ensemble : ensemble + 1] + gram_ref[p, :, ensemble + 1 : ensemble + 2]
        weights = times(z, times(z, pull)) / traces[p]
        transform_ref[p] = (z * jnp.sqrt((ensemble - 1.0) / traces[p]) + weights).astype(BF16)


def analyse(cells, transform):
    ensemble = cells.shape[1]
    ones = jnp.full((ensemble, ensemble), 1.0 / ensemble, BF16)
    mean = jnp.dot(cells, ones, preferred_element_type=F32)
    perturbation = (cells.astype(F32) - mean).astype(BF16)
    return (mean + jnp.dot(perturbation, transform, preferred_element_type=F32)).astype(BF16)


def sides(parity_ref, span):
    odd = parity_ref
    near = 1 - odd
    shift = (2 * near - 1).astype(F32) * span
    return near, shift


def centre_of(index):
    return jnp.asarray(2 * PATCH * index + PATCH, F32)


def mid_kernel(parity_ref, own_ref, first_ref, second_ref, state_ref, out_ref, gram, half, z, transform):
    ensemble = own_ref.shape[0] - EXTRA
    rows, cols = state_ref.shape[0], state_ref.shape[1]
    near, shift = sides(parity_ref[0], float(rows))
    row_index = (near, 1 - near)
    gram[...] = jnp.zeros_like(gram)
    inner = (1, 2)
    centres = [(centre_of(r), centre_of(c)) for r in row_index for c in inner]
    add_grams(gram, own_ref[...], (0.0, 0.0), (0, 1, 2, 3), centres, ensemble)
    add_grams(gram, first_ref[...], (shift, 0.0), (0, 1), centres, ensemble)
    add_grams(gram, second_ref[...], (-shift, 0.0), (2, 3), centres, ensemble)
    solve(gram, half, z, transform, 4, ensemble)
    for p in range(4):
        r, c = row_index[p // 2], inner[p % 2]
        at = pl.ds(pl.multiple_of(r * PATCH, PATCH), PATCH)
        cells = state_ref[at, c * PATCH : (c + 1) * PATCH, :].reshape(PATCH * PATCH, ensemble)
        out = analyse(cells, transform[p]).reshape(PATCH, PATCH, ensemble)
        out_ref[at, (c - 1) * PATCH : c * PATCH, :] = out


def edge_kernel(
    parity_ref, own_ref, first_ref, second_ref, near_ref, far_ref, state_ref, mid_ref, out_ref, gram, half, z, transform
):
    payload = own_ref.shape[0]
    ensemble = payload - EXTRA
    rows, cols = state_ref.shape[0], state_ref.shape[1]
    row_near, row_shift = sides(parity_ref[0], float(rows))
    col_near, col_shift = sides(parity_ref[1], float(cols))
    last = cols // PATCH - 1
    row_index = (row_near, 1 - row_near)
    col_index = (last * col_near, last * (1 - col_near))
    gram[...] = jnp.zeros_like(gram)
    centres = [(centre_of(r), centre_of(c)) for r in row_index for c in col_index]
    add_grams(gram, own_ref[...], (0.0, 0.0), (0, 1, 2, 3), centres, ensemble)
    add_grams(gram, first_ref[...], (row_shift, 0.0), (0, 1), centres, ensemble)
    add_grams(gram, second_ref[...], (-row_shift, 0.0), (2, 3), centres, ensemble)
    for at, (ref, shift) in enumerate(((near_ref, col_shift), (far_ref, -col_shift))):
        add_grams(gram, ref[:payload], (0.0, shift), (at, 2 + at), centres, ensemble)
        add_grams(gram, ref[payload : 2 * payload], (row_shift, shift), (at,), centres, ensemble)
        add_grams(gram, ref[2 * payload :], (-row_shift, shift), (2 + at,), centres, ensemble)
    solve(gram, half, z, transform, 4, ensemble)
    out_ref[:, PATCH : cols - PATCH, :] = mid_ref[...]
    for p in range(4):
        r, c = row_index[p // 2], col_index[p % 2]
        at = pl.ds(pl.multiple_of(r * PATCH, PATCH), PATCH)
        across = pl.ds(pl.multiple_of(c * PATCH, PATCH), PATCH)
        cells = state_ref[at, across, :].reshape(PATCH * PATCH, ensemble)
        out = analyse(cells, transform[p]).reshape(PATCH, PATCH, ensemble)
        out_ref[at, across, :] = out


def vmem(count):
    return [pl.BlockSpec(memory_space=pltpu.VMEM)] * count


SMEM = pl.BlockSpec(memory_space=pltpu.SMEM)


def scratch(ensemble):
    return [
        pltpu.VMEM((4, ensemble, ensemble + EXTRA), F32),
        pltpu.VMEM((4, ensemble, ensemble), F32),
        pltpu.VMEM((4, ensemble, ensemble), F32),
        pltpu.VMEM((4, ensemble, ensemble), BF16),
    ]


def pack(members, values, precision, cells, counts, tile_cols):
    capacity, ensemble = members.shape
    return pl.pallas_call(
        functools.partial(pack_kernel, tile_cols=tile_cols),
        out_shape=jax.ShapeDtypeStruct((ensemble + EXTRA, capacity), BF16),
        in_specs=[SMEM] + vmem(4),
        out_specs=pl.BlockSpec(memory_space=pltpu.VMEM),
    )(counts, members, values, precision, cells)


def middle(parity, own, first, second, state):
    rows, cols, ensemble = state.shape
    return pl.pallas_call(
        mid_kernel,
        out_shape=jax.ShapeDtypeStruct((rows, cols - 2 * PATCH, ensemble), BF16),
        in_specs=[SMEM] + vmem(4),
        out_specs=pl.BlockSpec(memory_space=pltpu.VMEM),
        scratch_shapes=scratch(ensemble),
        compiler_params=pltpu.CompilerParams(vmem_limit_bytes=24 << 20),
        cost_estimate=pl.CostEstimate(flops=1 << 32, bytes_accessed=1 << 20, transcendentals=0),
    )(parity, own, first, second, state)


def edges(parity, own, first, second, near, far, state, mid):
    return pl.pallas_call(
        edge_kernel,
        out_shape=jax.ShapeDtypeStruct(state.shape, BF16),
        in_specs=[SMEM] + vmem(7),
        out_specs=pl.BlockSpec(memory_space=pltpu.VMEM),
        scratch_shapes=scratch(state.shape[-1]),
        compiler_params=pltpu.CompilerParams(vmem_limit_bytes=24 << 20),
    )(parity, own, first, second, near, far, state, mid)


def exchange(x, axis, first, wrap):
    count = lax.axis_size(axis)
    pairs = []
    for low in range(first, count, 2):
        high = (low + 1) % count
        if high > low or wrap:
            pairs += [(low, high), (high, low)]
    return lax.ppermute(x, axis, pairs)


def body(state, obs_members, obs_values, obs_precision, obs_cells, obs_counts):
    _, tile_rows, tile_cols, ensemble = state.shape
    capacity = obs_members.shape[2]
    parity = jnp.stack([lax.axis_index("lat") % 2, lax.axis_index("lon") % 2]).astype(jnp.int32)
    own = pack(
        obs_members.reshape(capacity, ensemble),
        obs_values.reshape(1, capacity),
        obs_precision.reshape(1, capacity),
        obs_cells.reshape(1, capacity),
        obs_counts,
        tile_cols,
    )
    second = exchange(own, "lat", 1, False)
    first = exchange(own, "lat", 0, False)
    column = jnp.concatenate([own, first, second], axis=0)
    far = exchange(column, "lon", 1, True)
    near = exchange(column, "lon", 0, True)
    cells = state.reshape(tile_rows, tile_cols, ensemble)
    mid = middle(parity, own, first, second, cells)
    out = edges(parity, own, first, second, near, far, cells, mid)
    return out.reshape(state.shape)


def solution(mesh):
    in_specs = (
        P(None, "lat", "lon", None),
        P("lat", "lon", None, None),
        P("lat", "lon", None),
        P("lat", "lon", None),
        P("lat", "lon", None),
        P("lat", "lon"),
    )
    out_specs = P(None, "lat", "lon", None)
    return jax.shard_map(body, mesh=mesh, in_specs=in_specs, out_specs=out_specs, check_vma=False)
```

```python
import functools

import jax
import jax.numpy as jnp
from jax import lax
from jax.experimental import pallas as pl
from jax.experimental.pallas import tpu as pltpu
from jax.sharding import PartitionSpec as P

PATCH = 16
NS_STEPS = 12
RAD = 24
EXTRA = 16
WEIGHT, ROW, COL = 2, 5, 6
UNROLL = 10
F32, BF16 = jnp.float32, jnp.bfloat16


def halves(x):
    high = x.astype(BF16)
    return high, (x - high.astype(F32)).astype(BF16)


def thirds(x):
    high = x.astype(BF16)
    return high, *halves(x - high.astype(F32))


def side_by_side(x):
    return jnp.concatenate(halves(x), axis=1)


def pack_kernel(count_ref, members_in, values_in, precision_in, cells_in, out_ref, *scratch, tile_cols):
    *held, semaphores = scratch
    given = (members_in, values_in, precision_in, cells_in)
    copies = [pltpu.make_async_copy(a, b, semaphores.at[at]) for at, (a, b) in enumerate(zip(given, held))]
    for copy in copies:
        copy.start()
    for copy in copies:
        copy.wait()
    members_ref, values_ref, precision_ref, cells_ref = held
    capacity, ensemble = members_ref.shape
    members = members_ref[...].T.astype(F32)
    mean = jnp.sum(members, axis=0, keepdims=True) * (1.0 / ensemble)
    out_ref[:ensemble, :] = (members - mean).astype(BF16)
    slot = lax.broadcasted_iota(jnp.int32, (1, capacity), 1)
    weight = jnp.where(slot < count_ref[0, 0], precision_ref[...], 0.0)
    cells = cells_ref[...]
    rows = [
        *halves(values_ref[...] - mean),
        *thirds(weight),
        (cells // tile_cols).astype(BF16),
        (cells % tile_cols).astype(BF16),
    ]
    index = lax.broadcasted_iota(jnp.int32, (EXTRA, capacity), 0)
    extra = jnp.zeros((EXTRA, capacity), F32)
    for at, row in enumerate(rows):
        extra = jnp.where(index == at, row.astype(F32), extra)
    out_ref[ensemble:, :] = extra.astype(BF16)


def locals_of(scalars, row_shift, col_shift, centres):
    high, middle, low = (scalars[WEIGHT + at : WEIGHT + at + 1] for at in range(3))
    weight = high + (middle + low)
    rows_twice = 2.0 * (scalars[ROW : ROW + 1] + row_shift) + 1.0
    cols_twice = 2.0 * (scalars[COL : COL + 1] + col_shift) + 1.0
    count = len(centres)
    index = lax.broadcasted_iota(jnp.int32, (8, 1), 0)
    row_centre = jnp.zeros((8, 1), F32)
    col_centre = jnp.zeros((8, 1), F32)
    for at, (row, col) in enumerate(centres):
        row_centre = jnp.where(index == at, row, row_centre)
        col_centre = jnp.where(index == at, col, col_centre)
    row_gap = rows_twice - row_centre
    col_gap = cols_twice - col_centre
    distance = row_gap * row_gap + col_gap * col_gap
    taper = jnp.where(distance < 4.0 * RAD * RAD, jnp.exp(-distance / (2.0 * RAD * RAD)), 0.0)
    local = weight * taper
    return [local[at : at + 1] for at in range(count)]


def add_grams(gram_ref, payload, shifts, patches, centres, ensemble):
    scalars = payload[ensemble:].astype(F32)
    spread = payload[:ensemble].astype(F32)
    local = locals_of(scalars, *shifts, [centres[p] for p in patches])
    weighted = jnp.concatenate([(row * spread).astype(BF16) for row in local], axis=0)
    part = lax.dot_general(weighted, payload, (((1,), (1,)), ((), ())), preferred_element_type=F32)
    for at, p in enumerate(patches):
        gram_ref[p] += part[at * ensemble : (at + 1) * ensemble]


def double_dot(left, right):
    width = right.shape[1] // 2
    both = jnp.dot(left, jnp.concatenate([right, right], axis=0), preferred_element_type=F32)
    return both[:, :width] + both[:, width:]


def solve(gram_ref, half_ref, z_ref, right_ref, transform_ref, ensemble):
    patches = range(gram_ref.shape[0])
    row = lax.broadcasted_iota(jnp.int32, (ensemble, ensemble), 0)
    col = lax.broadcasted_iota(jnp.int32, (ensemble, ensemble), 1)
    diagonal = row == col
    traces = []
    for p in patches:
        system = gram_ref[p, :, :ensemble] + jnp.where(diagonal, ensemble - 1.0, 0.0)
        on = jnp.where(diagonal, system, 0.0)
        trace = jnp.sum(jnp.sum(on, axis=0, keepdims=True), axis=1, keepdims=True)
        traces.append(trace)
        half = system * (-0.5 / trace)
        half_ref[p] = half
        right_ref[p] = side_by_side(half)
        z_ref[p] = jnp.where(diagonal, 1.5, 0.0) + half

    def times(matrix, column):
        across = jnp.sum(jnp.where(diagonal, column, 0.0), axis=0, keepdims=True)
        return jnp.sum(matrix * across, axis=1, keepdims=True)

    def advance(with_root):
        for p in patches:
            right = right_ref[p]
            if with_root:
                z = z_ref[p]
                both = double_dot(jnp.concatenate([right, side_by_side(z)], axis=0), right)
                z_ref[p] = 1.5 * z + both[ensemble:]
            else:
                both = double_dot(right, right)
            half_ref[p] = 1.5 * half_ref[p] + both[:ensemble]
        for p in patches:
            middle = half_ref[p]
            half = 1.5 * middle + double_dot(side_by_side(middle), right_ref[p])
            half_ref[p] = half
            right_ref[p] = side_by_side(half)

    def step(_, carry):
        advance(True)
        return carry

    advance(False)
    lax.fori_loop(0, NS_STEPS - 2, step, 0, unroll=UNROLL)
    for p in patches:
        z = z_ref[p]
        z_ref[p] = 1.5 * z + double_dot(side_by_side(z), right_ref[p])
    pulls = [gram_ref[p, :, ensemble : ensemble + 1] + gram_ref[p, :, ensemble + 1 : ensemble + 2] for p in patches]
    inner = [times(z_ref[p], pulls[p]) for p in patches]
    weights = [times(z_ref[p], inner[p]) for p in patches]
    for p in patches:
        scale = jnp.sqrt((ensemble - 1.0) / traces[p])
        transform_ref[p] = (z_ref[p] * scale + weights[p] / traces[p]).astype(BF16)


def analyse(cells, transform):
    ensemble = cells.shape[1]
    ones = jnp.full((ensemble, ensemble), 1.0 / ensemble, BF16)
    mean = jnp.dot(cells, ones, preferred_element_type=F32)
    perturbation = (cells.astype(F32) - mean).astype(BF16)
    return (mean + jnp.dot(perturbation, transform, preferred_element_type=F32)).astype(BF16)


def sides(parity_ref, span):
    odd = parity_ref
    near = 1 - odd
    shift = (2 * near - 1).astype(F32) * span
    return near, shift


def centre_of(index):
    return jnp.asarray(2 * PATCH * index + PATCH, F32)


def mid_kernel(parity_ref, own_ref, second_ref, first_ref, state_ref, out_ref, gram, half, z, right, transform):
    ensemble = own_ref.shape[0] - EXTRA
    rows, cols = state_ref.shape[0], state_ref.shape[1]
    near, shift = sides(parity_ref[0], float(rows))
    row_index = (near, 1 - near)
    gram[...] = jnp.zeros_like(gram)
    inner = (1, 2)
    centres = [(centre_of(r), centre_of(c)) for r in row_index for c in inner]
    add_grams(gram, own_ref[...], (0.0, 0.0), (0, 1, 2, 3), centres, ensemble)
    add_grams(gram, first_ref[...], (shift, 0.0), (0, 1), centres, ensemble)
    add_grams(gram, second_ref[...], (-shift, 0.0), (2, 3), centres, ensemble)
    solve(gram, half, z, right, transform, ensemble)
    for p in range(4):
        r, c = row_index[p // 2], inner[p % 2]
        at = pl.ds(pl.multiple_of(r * PATCH, PATCH), PATCH)
        cells = state_ref[at, c * PATCH : (c + 1) * PATCH, :].reshape(PATCH * PATCH, ensemble)
        out = analyse(cells, transform[p]).reshape(PATCH, PATCH, ensemble)
        out_ref[at, (c - 1) * PATCH : c * PATCH, :] = out


def edge_kernel(
    parity_ref, own_ref, second_ref, first_ref, near_ref, far_ref, state_ref, mid_ref, out_ref, gram, half, z, right, transform, done, semaphores
):
    payload = own_ref.shape[0]
    ensemble = payload - EXTRA
    rows, cols = state_ref.shape[0], state_ref.shape[1]
    inner = pltpu.make_async_copy(mid_ref, out_ref.at[:, PATCH : cols - PATCH, :], semaphores.at[4])
    inner.start()
    row_near, row_shift = sides(parity_ref[0], float(rows))
    col_near, col_shift = sides(parity_ref[1], float(cols))
    last = cols // PATCH - 1
    row_index = (row_near, 1 - row_near)
    col_index = (last * col_near, last * (1 - col_near))
    gram[...] = jnp.zeros_like(gram)
    centres = [(centre_of(r), centre_of(c)) for r in row_index for c in col_index]
    add_grams(gram, own_ref[...], (0.0, 0.0), (0, 1, 2, 3), centres, ensemble)
    add_grams(gram, first_ref[...], (row_shift, 0.0), (0, 1), centres, ensemble)
    add_grams(gram, second_ref[...], (-row_shift, 0.0), (2, 3), centres, ensemble)
    for at, (ref, shift) in enumerate(((near_ref, col_shift), (far_ref, -col_shift))):
        add_grams(gram, ref[:payload], (0.0, shift), (at, 2 + at), centres, ensemble)
        add_grams(gram, ref[payload : 2 * payload], (row_shift, shift), (at,), centres, ensemble)
        add_grams(gram, ref[2 * payload :], (-row_shift, shift), (2 + at,), centres, ensemble)
    solve(gram, half, z, right, transform, ensemble)
    copies = []
    for p in range(4):
        r, c = row_index[p // 2], col_index[p % 2]
        at = pl.ds(pl.multiple_of(r * PATCH, PATCH), PATCH)
        across = pl.ds(pl.multiple_of(c * PATCH, PATCH), PATCH)
        cells = state_ref[at, across, :].reshape(PATCH * PATCH, ensemble)
        done[p] = analyse(cells, transform[p]).reshape(PATCH, PATCH, ensemble)
        copies.append(pltpu.make_async_copy(done.at[p], out_ref.at[at, across, :], semaphores.at[p]))
        copies[p].start()
    for copy in (inner, *copies):
        copy.wait()


def vmem(count):
    return [pl.BlockSpec(memory_space=pltpu.VMEM)] * count


SMEM = pl.BlockSpec(memory_space=pltpu.SMEM)


def scratch(ensemble):
    return [
        pltpu.VMEM((4, ensemble, ensemble + EXTRA), F32),
        pltpu.VMEM((4, ensemble, ensemble), F32),
        pltpu.VMEM((4, ensemble, ensemble), F32),
        pltpu.VMEM((4, ensemble, 2 * ensemble), BF16),
        pltpu.VMEM((4, ensemble, ensemble), BF16),
    ]


def pack(members, values, precision, cells, counts, tile_cols):
    capacity, ensemble = members.shape
    given = [pltpu.with_memory_space_constraint(x, pltpu.HBM) for x in (members, values, precision, cells)]
    return pl.pallas_call(
        functools.partial(pack_kernel, tile_cols=tile_cols),
        out_shape=pltpu.VMEM((ensemble + EXTRA, capacity), BF16),
        in_specs=[SMEM] + [pl.BlockSpec(memory_space=pltpu.HBM)] * len(given),
        out_specs=pl.BlockSpec(memory_space=pltpu.VMEM),
        scratch_shapes=[pltpu.VMEM(x.shape, x.dtype) for x in given] + [pltpu.SemaphoreType.DMA((len(given),))],
        compiler_params=pltpu.CompilerParams(vmem_limit_bytes=4 << 20),
    )(counts, *given)


def stack_kernel(own_ref, second_ref, first_ref, out_ref):
    rows = own_ref.shape[0]
    for at, ref in enumerate((own_ref, first_ref, second_ref)):
        out_ref[at * rows : (at + 1) * rows, :] = ref[...]


def stack(own, first, second):
    rows, capacity = own.shape
    return pl.pallas_call(
        stack_kernel,
        out_shape=jax.ShapeDtypeStruct((3 * rows, capacity), BF16),
        in_specs=vmem(3),
        out_specs=pl.BlockSpec(memory_space=pltpu.VMEM),
        compiler_params=pltpu.CompilerParams(vmem_limit_bytes=4 << 20),
    )(own, second, first)


def middle(parity, own, first, second, state):
    rows, cols, ensemble = state.shape
    return pl.pallas_call(
        mid_kernel,
        out_shape=jax.ShapeDtypeStruct((rows, cols - 2 * PATCH, ensemble), BF16),
        in_specs=[SMEM] + vmem(4),
        out_specs=pl.BlockSpec(memory_space=pltpu.VMEM),
        scratch_shapes=scratch(ensemble),
        compiler_params=pltpu.CompilerParams(vmem_limit_bytes=12 << 20),
        cost_estimate=pl.CostEstimate(flops=1 << 32, bytes_accessed=1 << 20, transcendentals=0),
    )(parity, own, second, first, state)


def edges(parity, own, first, second, near, far, state, mid):
    ensemble = state.shape[-1]
    return pl.pallas_call(
        edge_kernel,
        out_shape=jax.ShapeDtypeStruct(state.shape, BF16),
        in_specs=[SMEM] + vmem(7),
        out_specs=pl.BlockSpec(memory_space=pltpu.HBM),
        scratch_shapes=scratch(ensemble)
        + [pltpu.VMEM((4, PATCH, PATCH, ensemble), BF16), pltpu.SemaphoreType.DMA((5,))],
        compiler_params=pltpu.CompilerParams(vmem_limit_bytes=12 << 20),
    )(parity, own, second, first, near, far, state, mid)


def exchange(x, axis, first, wrap):
    count = lax.axis_size(axis)
    pairs = []
    for low in range(first, count, 2):
        high = (low + 1) % count
        if high > low or wrap:
            pairs += [(low, high), (high, low)]
    return lax.ppermute(x, axis, pairs)


def body(state, obs_members, obs_values, obs_precision, obs_cells, obs_counts):
    _, tile_rows, tile_cols, ensemble = state.shape
    capacity = obs_members.shape[2]
    parity = jnp.stack([lax.axis_index("lat") % 2, lax.axis_index("lon") % 2]).astype(jnp.int32)
    own = pack(
        obs_members.reshape(capacity, ensemble),
        obs_values.reshape(1, capacity),
        obs_precision.reshape(1, capacity),
        obs_cells.reshape(1, capacity),
        obs_counts,
        tile_cols,
    )
    first = exchange(own, "lat", 0, False)
    second = exchange(own, "lat", 1, False)
    column = stack(own, first, second)
    far = exchange(column, "lon", 1, True)
    near = exchange(column, "lon", 0, True)
    cells = state.reshape(tile_rows, tile_cols, ensemble)
    mid = middle(parity, own, first, second, cells)
    out = edges(parity, own, first, second, near, far, cells, mid)
    return out.reshape(state.shape)


def solution(mesh):
    in_specs = (
        P(None, "lat", "lon", None),
        P("lat", "lon", None, None),
        P("lat", "lon", None),
        P("lat", "lon", None),
        P("lat", "lon", None),
        P("lat", "lon"),
    )
    out_specs = P(None, "lat", "lon", None)
    return jax.shard_map(body, mesh=mesh, in_specs=in_specs, out_specs=out_specs, check_vma=False)
```

```python
import functools

import jax
import jax.numpy as jnp
from jax import lax
from jax.experimental import pallas as pl
from jax.experimental.pallas import tpu as pltpu
from jax.sharding import PartitionSpec as P

PATCH = 16
NS_STEPS = 12
RAD = 24
EXTRA = 16
WEIGHT, ROW, COL = 2, 5, 6
UNROLL = 10
BLOCKS = 4
F32, BF16 = jnp.float32, jnp.bfloat16


def halves(x):
    high = x.astype(BF16)
    return high, (x - high.astype(F32)).astype(BF16)


def thirds(x):
    high = x.astype(BF16)
    return high, *halves(x - high.astype(F32))


def side_by_side(x):
    return jnp.concatenate(halves(x), axis=1)


def pack_kernel(count_ref, members_in, values_in, precision_in, cells_in, out_ref, *scratch, tile_cols):
    *held, semaphores = scratch
    given = (members_in, values_in, precision_in, cells_in)
    copies = [pltpu.make_async_copy(a, b, semaphores.at[at]) for at, (a, b) in enumerate(zip(given, held))]
    for copy in copies:
        copy.start()
    for copy in copies:
        copy.wait()
    members_ref, values_ref, precision_ref, cells_ref = held
    capacity, ensemble = members_ref.shape
    members = members_ref[...].T.astype(F32)
    mean = jnp.sum(members, axis=0, keepdims=True) * (1.0 / ensemble)
    out_ref[:ensemble, :] = (members - mean).astype(BF16)
    slot = lax.broadcasted_iota(jnp.int32, (1, capacity), 1)
    weight = jnp.where(slot < count_ref[0, 0], precision_ref[...], 0.0)
    cells = cells_ref[...]
    rows = [
        *halves(values_ref[...] - mean),
        *thirds(weight),
        (cells // tile_cols).astype(BF16),
        (cells % tile_cols).astype(BF16),
    ]
    index = lax.broadcasted_iota(jnp.int32, (EXTRA, capacity), 0)
    extra = jnp.zeros((EXTRA, capacity), F32)
    for at, row in enumerate(rows):
        extra = jnp.where(index == at, row.astype(F32), extra)
    out_ref[ensemble:, :] = extra.astype(BF16)


def locals_of(scalars, row_shift, col_shift, centres):
    high, middle, low = (scalars[WEIGHT + at : WEIGHT + at + 1] for at in range(3))
    weight = high + (middle + low)
    rows_twice = 2.0 * (scalars[ROW : ROW + 1] + row_shift) + 1.0
    cols_twice = 2.0 * (scalars[COL : COL + 1] + col_shift) + 1.0
    count = len(centres)
    index = lax.broadcasted_iota(jnp.int32, (8, 1), 0)
    row_centre = jnp.zeros((8, 1), F32)
    col_centre = jnp.zeros((8, 1), F32)
    for at, (row, col) in enumerate(centres):
        row_centre = jnp.where(index == at, row, row_centre)
        col_centre = jnp.where(index == at, col, col_centre)
    row_gap = rows_twice - row_centre
    col_gap = cols_twice - col_centre
    distance = row_gap * row_gap + col_gap * col_gap
    taper = jnp.where(distance < 4.0 * RAD * RAD, jnp.exp(-distance / (2.0 * RAD * RAD)), 0.0)
    local = weight * taper
    return [local[at : at + 1] for at in range(count)]


def add_grams(gram_refs, payload, shifts, centres):
    ensemble = payload.shape[0] - EXTRA
    spread = payload[:ensemble].astype(F32)
    local = locals_of(payload[ensemble:].astype(F32), *shifts, centres)
    weighted = jnp.concatenate([(row * spread).astype(BF16) for row in local], axis=0)
    part = lax.dot_general(weighted, payload, (((1,), (1,)), ((), ())), preferred_element_type=F32)
    for at, ref in enumerate(gram_refs):
        ref[...] += part[at * ensemble : (at + 1) * ensemble]


def add_column(gram_refs, column_ref, col_shift, centres, tile_rows):
    payload = column_ref.shape[0] // BLOCKS
    half = len(gram_refs) // 2
    upper, lower = slice(0, half), slice(half, None)
    blocks = [column_ref[at * payload : (at + 1) * payload, :] for at in range(BLOCKS)]
    add_grams(gram_refs, blocks[0], (0.0, col_shift), centres)
    add_grams(gram_refs[upper], blocks[1], (-tile_rows, col_shift), centres[upper])
    add_grams(gram_refs[lower], blocks[2], (tile_rows, col_shift), centres[lower])
    add_grams(gram_refs, blocks[3], (0.0, col_shift), centres)


def double_dot(left, right):
    width = right.shape[1] // 2
    both = jnp.dot(left, jnp.concatenate([right, right], axis=0), preferred_element_type=F32)
    return both[:, :width] + both[:, width:]


def solve(gram_ref, half_ref, z_ref, right_ref, transform_ref, ensemble):
    patches = range(gram_ref.shape[0])
    row = lax.broadcasted_iota(jnp.int32, (ensemble, ensemble), 0)
    col = lax.broadcasted_iota(jnp.int32, (ensemble, ensemble), 1)
    diagonal = row == col
    traces = []
    for p in patches:
        system = gram_ref[p, :, :ensemble] + jnp.where(diagonal, ensemble - 1.0, 0.0)
        on = jnp.where(diagonal, system, 0.0)
        trace = jnp.sum(jnp.sum(on, axis=0, keepdims=True), axis=1, keepdims=True)
        traces.append(trace)
        half = system * (-0.5 / trace)
        half_ref[p] = half
        right_ref[p] = side_by_side(half)
        z_ref[p] = jnp.where(diagonal, 1.5, 0.0) + half

    def times(matrix, column):
        across = jnp.sum(jnp.where(diagonal, column, 0.0), axis=0, keepdims=True)
        return jnp.sum(matrix * across, axis=1, keepdims=True)

    def advance(with_root):
        for p in patches:
            right = right_ref[p]
            if with_root:
                z = z_ref[p]
                both = double_dot(jnp.concatenate([right, side_by_side(z)], axis=0), right)
                z_ref[p] = 1.5 * z + both[ensemble:]
            else:
                both = double_dot(right, right)
            half_ref[p] = 1.5 * half_ref[p] + both[:ensemble]
        for p in patches:
            middle = half_ref[p]
            half = 1.5 * middle + double_dot(side_by_side(middle), right_ref[p])
            half_ref[p] = half
            right_ref[p] = side_by_side(half)

    def step(_, carry):
        advance(True)
        return carry

    advance(False)
    lax.fori_loop(0, NS_STEPS - 2, step, 0, unroll=UNROLL)
    for p in patches:
        z = z_ref[p]
        z_ref[p] = 1.5 * z + double_dot(side_by_side(z), right_ref[p])
    pulls = [gram_ref[p, :, ensemble : ensemble + 1] + gram_ref[p, :, ensemble + 1 : ensemble + 2] for p in patches]
    inner = [times(z_ref[p], pulls[p]) for p in patches]
    weights = [times(z_ref[p], inner[p]) for p in patches]
    for p in patches:
        scale = jnp.sqrt((ensemble - 1.0) / traces[p])
        transform_ref[p] = (z_ref[p] * scale + weights[p] / traces[p]).astype(BF16)


def analyse(cells, transform):
    ensemble = cells.shape[1]
    ones = jnp.full((ensemble, ensemble), 1.0 / ensemble, BF16)
    mean = jnp.dot(cells, ones, preferred_element_type=F32)
    perturbation = (cells.astype(F32) - mean).astype(BF16)
    return (mean + jnp.dot(perturbation, transform, preferred_element_type=F32)).astype(BF16)


def sides(odd, cols):
    last = cols // PATCH - 1
    shift = (1 - 2 * odd).astype(F32) * cols
    return (last * (1 - odd), last * odd), shift


def centre_of(index):
    return jnp.asarray(2 * PATCH * index + PATCH, F32)


def patch_at(r, c):
    return pl.ds(r * PATCH, PATCH), pl.ds(pl.multiple_of(c * PATCH, PATCH), PATCH)


def centres_of(columns):
    return [(centre_of(r), centre_of(c)) for r in range(2) for c in columns]


def mid_kernel(odd_ref, column_ref, state_ref, out_ref, part_ref, gram, half, z, right, transform):
    rows, cols, ensemble = state_ref.shape
    inner = (1, 2)
    edge_columns, _ = sides(odd_ref[0], cols)
    gram[...] = jnp.zeros_like(gram)
    part_ref[...] = jnp.zeros_like(part_ref)
    refs = [ref.at[2 * r + at] for r in range(2) for ref in (gram, part_ref) for at in range(2)]
    add_column(refs, column_ref, 0.0, centres_of(inner + edge_columns), float(rows))
    solve(gram, half, z, right, transform, ensemble)
    for p in range(4):
        at, across = patch_at(p // 2, inner[p % 2])
        cells = state_ref[at, across, :].reshape(PATCH * PATCH, ensemble)
        out = analyse(cells, transform[p]).reshape(PATCH, PATCH, ensemble)
        out_ref[at, pl.ds((p % 2) * PATCH, PATCH), :] = out


def edge_kernel(odd_ref, near_ref, far_ref, state_ref, mid_ref, part_ref, out_ref, gram, half, z, right, transform, done, semaphores):
    rows, cols, ensemble = state_ref.shape
    inner = pltpu.make_async_copy(mid_ref, out_ref.at[:, PATCH : cols - PATCH, :], semaphores.at[4])
    inner.start()
    edge_columns, shift = sides(odd_ref[0], cols)
    gram[...] = part_ref[...]
    for at, (ref, col_shift) in enumerate(((near_ref, shift), (far_ref, -shift))):
        refs = [gram.at[at], gram.at[2 + at]]
        add_column(refs, ref, col_shift, centres_of(edge_columns[at : at + 1]), float(rows))
    solve(gram, half, z, right, transform, ensemble)
    copies = []
    for p in range(4):
        at, across = patch_at(p // 2, edge_columns[p % 2])
        cells = state_ref[at, across, :].reshape(PATCH * PATCH, ensemble)
        done[p] = analyse(cells, transform[p]).reshape(PATCH, PATCH, ensemble)
        copies.append(pltpu.make_async_copy(done.at[p], out_ref.at[at, across, :], semaphores.at[p]))
        copies[p].start()
    for copy in (inner, *copies):
        copy.wait()


def vmem(count):
    return [pl.BlockSpec(memory_space=pltpu.VMEM)] * count


SMEM = pl.BlockSpec(memory_space=pltpu.SMEM)


def scratch(ensemble):
    return [
        pltpu.VMEM((4, ensemble, ensemble + EXTRA), F32),
        pltpu.VMEM((4, ensemble, ensemble), F32),
        pltpu.VMEM((4, ensemble, ensemble), F32),
        pltpu.VMEM((4, ensemble, 2 * ensemble), BF16),
        pltpu.VMEM((4, ensemble, ensemble), BF16),
    ]


def pack(members, values, precision, cells, counts, tile_cols):
    capacity, ensemble = members.shape
    given = [pltpu.with_memory_space_constraint(x, pltpu.HBM) for x in (members, values, precision, cells)]
    return pl.pallas_call(
        functools.partial(pack_kernel, tile_cols=tile_cols),
        out_shape=pltpu.VMEM((ensemble + EXTRA, capacity), BF16),
        in_specs=[SMEM] + [pl.BlockSpec(memory_space=pltpu.HBM)] * len(given),
        out_specs=pl.BlockSpec(memory_space=pltpu.VMEM),
        scratch_shapes=[pltpu.VMEM(x.shape, x.dtype) for x in given] + [pltpu.SemaphoreType.DMA((len(given),))],
        compiler_params=pltpu.CompilerParams(vmem_limit_bytes=4 << 20),
    )(counts, *given)


def stack_kernel(own_ref, south_ref, north_ref, out_ref, *, tile_rows):
    rows, capacity = own_ref.shape
    kept = capacity // 2
    ensemble = rows - EXTRA
    tiles = (own_ref, north_ref, south_ref)
    for at, ref in enumerate(tiles):
        out_ref[at * rows : (at + 1) * rows, :] = ref[:, :kept]
    full = [
        jnp.max(ref[ensemble:, kept:].astype(F32)[WEIGHT : WEIGHT + 1], axis=1, keepdims=True) > 0.0 for ref in tiles[:2]
    ]

    def chosen(own, north, south):
        return jnp.where(full[0], own, jnp.where(full[1], north, south))

    spreads = [ref[:ensemble, kept:].astype(F32) for ref in tiles]
    scalars = [ref[ensemble:, kept:].astype(F32) for ref in tiles]
    index = lax.broadcasted_iota(jnp.int32, (EXTRA, kept), 0)
    shift = chosen(0.0, -float(tile_rows), float(tile_rows))
    out_ref[3 * rows : 3 * rows + ensemble, :] = chosen(*spreads).astype(BF16)
    out_ref[3 * rows + ensemble :, :] = (chosen(*scalars) + jnp.where(index == ROW, shift, 0.0)).astype(BF16)


def stack(own, north, south, tile_rows):
    rows, capacity = own.shape
    return pl.pallas_call(
        functools.partial(stack_kernel, tile_rows=tile_rows),
        out_shape=pltpu.VMEM((BLOCKS * rows, capacity // 2), BF16),
        in_specs=vmem(3),
        out_specs=pl.BlockSpec(memory_space=pltpu.VMEM),
        compiler_params=pltpu.CompilerParams(vmem_limit_bytes=4 << 20),
    )(own, south, north)


def middle(odd, column, state):
    rows, cols, ensemble = state.shape
    return pl.pallas_call(
        mid_kernel,
        out_shape=(
            pltpu.VMEM((rows, cols - 2 * PATCH, ensemble), BF16),
            pltpu.VMEM((4, ensemble, ensemble + EXTRA), F32),
        ),
        in_specs=[SMEM] + vmem(2),
        out_specs=tuple(vmem(2)),
        scratch_shapes=scratch(ensemble),
        compiler_params=pltpu.CompilerParams(vmem_limit_bytes=12 << 20),
        cost_estimate=pl.CostEstimate(flops=1 << 32, bytes_accessed=1 << 20, transcendentals=0),
    )(odd, column, state)


def edges(odd, near, far, state, mid, part):
    ensemble = state.shape[-1]
    return pl.pallas_call(
        edge_kernel,
        out_shape=jax.ShapeDtypeStruct(state.shape, BF16),
        in_specs=[SMEM] + vmem(5),
        out_specs=pl.BlockSpec(memory_space=pltpu.HBM),
        scratch_shapes=scratch(ensemble)
        + [pltpu.VMEM((4, PATCH, PATCH, ensemble), BF16), pltpu.SemaphoreType.DMA((5,))],
        compiler_params=pltpu.CompilerParams(vmem_limit_bytes=12 << 20),
    )(odd, near, far, state, mid, part)


def shifted(x, axis, step):
    count = lax.axis_size(axis)
    return lax.ppermute(x, axis, [(i, i + step) for i in range(count) if 0 <= i + step < count])


def exchange(x, axis, first):
    count = lax.axis_size(axis)
    pairs = []
    for low in range(first, count, 2):
        high = (low + 1) % count
        pairs += [(low, high), (high, low)]
    return lax.ppermute(x, axis, pairs)


def body(state, obs_members, obs_values, obs_precision, obs_cells, obs_counts):
    _, tile_rows, tile_cols, ensemble = state.shape
    capacity = obs_members.shape[2]
    odd = (lax.axis_index("lon") & 1).astype(jnp.int32).reshape(1)
    own = pack(
        obs_members.reshape(capacity, ensemble),
        obs_values.reshape(1, capacity),
        obs_precision.reshape(1, capacity),
        obs_cells.reshape(1, capacity),
        obs_counts,
        tile_cols,
    )
    north = shifted(own, "lat", 1)
    south = shifted(own, "lat", -1)
    column = stack(own, north, south, tile_rows)
    far = exchange(column, "lon", 1)
    near = exchange(column, "lon", 0)
    cells = state.reshape(tile_rows, tile_cols, ensemble)
    mid, part = middle(odd, column, cells)
    out = edges(odd, near, far, cells, mid, part)
    return out.reshape(state.shape)


def solution(mesh):
    in_specs = (
        P(None, "lat", "lon", None),
        P("lat", "lon", None, None),
        P("lat", "lon", None),
        P("lat", "lon", None),
        P("lat", "lon", None),
        P("lat", "lon"),
    )
    out_specs = P(None, "lat", "lon", None)
    return jax.shard_map(body, mesh=mesh, in_specs=in_specs, out_specs=out_specs, check_vma=False)
```

```python
import functools

import jax
import jax.numpy as jnp
from jax import lax
from jax.experimental import pallas as pl
from jax.experimental.pallas import tpu as pltpu
from jax.sharding import PartitionSpec as P

PATCH = 16
NS_STEPS = 12
RAD = 24
EXTRA = 16
WEIGHT, ROW, COL = 2, 5, 6
UNROLL = 10
INNER = (1, 2)
BLOCKS = 4
F32, BF16 = jnp.float32, jnp.bfloat16


def halves(x):
    high = x.astype(BF16)
    return high, (x - high.astype(F32)).astype(BF16)


def thirds(x):
    high = x.astype(BF16)
    return high, *halves(x - high.astype(F32))


def side_by_side(x):
    return jnp.concatenate(halves(x), axis=1)


def pack_kernel(count_ref, members_in, values_in, precision_in, cells_in, out_ref, *scratch, tile_cols):
    *held, semaphores = scratch
    given = (members_in, values_in, precision_in, cells_in)
    copies = [pltpu.make_async_copy(a, b, semaphores.at[at]) for at, (a, b) in enumerate(zip(given, held))]
    for copy in copies:
        copy.start()
    for copy in copies:
        copy.wait()
    members_ref, values_ref, precision_ref, cells_ref = held
    capacity, ensemble = members_ref.shape
    members = members_ref[...].T.astype(F32)
    mean = jnp.sum(members, axis=0, keepdims=True) * (1.0 / ensemble)
    out_ref[:ensemble, :] = (members - mean).astype(BF16)
    slot = lax.broadcasted_iota(jnp.int32, (1, capacity), 1)
    weight = jnp.where(slot < count_ref[0, 0], precision_ref[...], 0.0)
    cells = cells_ref[...]
    rows = [
        *halves(values_ref[...] - mean),
        *thirds(weight),
        (cells // tile_cols).astype(BF16),
        (cells % tile_cols).astype(BF16),
    ]
    index = lax.broadcasted_iota(jnp.int32, (EXTRA, capacity), 0)
    extra = jnp.zeros((EXTRA, capacity), F32)
    for at, row in enumerate(rows):
        extra = jnp.where(index == at, row.astype(F32), extra)
    out_ref[ensemble:, :] = extra.astype(BF16)


def locals_of(scalars, row_shift, col_shift, centres):
    high, middle, low = (scalars[WEIGHT + at : WEIGHT + at + 1] for at in range(3))
    weight = high + (middle + low)
    rows_twice = 2.0 * (scalars[ROW : ROW + 1] + row_shift) + 1.0
    cols_twice = 2.0 * (scalars[COL : COL + 1] + col_shift) + 1.0
    count = len(centres)
    index = lax.broadcasted_iota(jnp.int32, (8, 1), 0)
    row_centre = jnp.zeros((8, 1), F32)
    col_centre = jnp.zeros((8, 1), F32)
    for at, (row, col) in enumerate(centres):
        row_centre = jnp.where(index == at, row, row_centre)
        col_centre = jnp.where(index == at, col, col_centre)
    row_gap = rows_twice - row_centre
    col_gap = cols_twice - col_centre
    distance = row_gap * row_gap + col_gap * col_gap
    taper = jnp.where(distance < 4.0 * RAD * RAD, jnp.exp(-distance / (2.0 * RAD * RAD)), 0.0)
    local = weight * taper
    return [local[at : at + 1] for at in range(count)]


def add_grams(gram_refs, payload, shifts, centres):
    ensemble = payload.shape[0] - EXTRA
    spread = payload[:ensemble].astype(F32)
    local = locals_of(payload[ensemble:].astype(F32), *shifts, centres)
    weighted = jnp.concatenate([(row * spread).astype(BF16) for row in local], axis=0)
    part = lax.dot_general(weighted, payload, (((1,), (1,)), ((), ())), preferred_element_type=F32)
    for at, ref in enumerate(gram_refs):
        ref[...] += part[at * ensemble : (at + 1) * ensemble]


def add_column(gram_refs, column_ref, col_shift, centres, tile_rows, own=True):
    payload = column_ref.shape[0] // BLOCKS
    half = len(gram_refs) // 2
    upper, lower = slice(0, half), slice(half, None)
    blocks = [column_ref[at * payload : (at + 1) * payload, :] for at in range(BLOCKS)]
    if own:
        add_grams(gram_refs, blocks[0], (0.0, col_shift), centres)
    add_grams(gram_refs[upper], blocks[1], (-tile_rows, col_shift), centres[upper])
    add_grams(gram_refs[lower], blocks[2], (tile_rows, col_shift), centres[lower])
    add_grams(gram_refs, blocks[3], (0.0, col_shift), centres)


def double_dot(left, right):
    width = right.shape[1] // 2
    both = jnp.dot(left, jnp.concatenate([right, right], axis=0), preferred_element_type=F32)
    return both[:, :width] + both[:, width:]


def solve(gram_ref, half_ref, z_ref, right_ref, transform_ref, ensemble):
    patches = range(gram_ref.shape[0])
    row = lax.broadcasted_iota(jnp.int32, (ensemble, ensemble), 0)
    col = lax.broadcasted_iota(jnp.int32, (ensemble, ensemble), 1)
    diagonal = row == col
    traces = []
    for p in patches:
        system = gram_ref[p, :, :ensemble] + jnp.where(diagonal, ensemble - 1.0, 0.0)
        on = jnp.where(diagonal, system, 0.0)
        trace = jnp.sum(jnp.sum(on, axis=0, keepdims=True), axis=1, keepdims=True)
        traces.append(trace)
        half = system * (-0.5 / trace)
        half_ref[p] = half
        right_ref[p] = side_by_side(half)
        z_ref[p] = jnp.where(diagonal, 1.5, 0.0) + half

    def times(matrix, column):
        across = jnp.sum(jnp.where(diagonal, column, 0.0), axis=0, keepdims=True)
        return jnp.sum(matrix * across, axis=1, keepdims=True)

    def first(p, with_root):
        right = right_ref[p]
        if with_root:
            z = z_ref[p]
            both = double_dot(jnp.concatenate([right, side_by_side(z)], axis=0), right)
            z_ref[p] = 1.5 * z + both[ensemble:]
        else:
            both = double_dot(right, right)
        half_ref[p] = 1.5 * half_ref[p] + both[:ensemble]

    def second(p):
        middle = half_ref[p]
        half = 1.5 * middle + double_dot(side_by_side(middle), right_ref[p])
        half_ref[p] = half
        right_ref[p] = side_by_side(half)

    def advance(with_root):
        split = len(patches) // 2
        for p in patches[:split]:
            first(p, with_root)
        for p in patches[split:]:
            first(p, with_root)
            second(p - split)
        for p in patches[split:]:
            second(p)

    def step(_, carry):
        advance(True)
        return carry

    advance(False)
    lax.fori_loop(0, NS_STEPS - 2, step, 0, unroll=UNROLL)
    for p in patches:
        z = z_ref[p]
        z_ref[p] = 1.5 * z + double_dot(side_by_side(z), right_ref[p])
    pulls = [gram_ref[p, :, ensemble : ensemble + 1] + gram_ref[p, :, ensemble + 1 : ensemble + 2] for p in patches]
    inner = [times(z_ref[p], pulls[p]) for p in patches]
    weights = [times(z_ref[p], inner[p]) for p in patches]
    for p in patches:
        scale = jnp.sqrt((ensemble - 1.0) / traces[p])
        transform_ref[p] = (z_ref[p] * scale + weights[p] / traces[p]).astype(BF16)


def centred(cells):
    ensemble = cells.shape[1]
    ones = jnp.full((ensemble, ensemble), 1.0 / ensemble, BF16)
    mean = jnp.dot(cells, ones, preferred_element_type=F32)
    return mean, (cells.astype(F32) - mean).astype(BF16)


def sides(odd, cols):
    last = cols // PATCH - 1
    shift = (1 - 2 * odd).astype(F32) * cols
    return (last * (1 - odd), last * odd), shift


def centre_of(index):
    return jnp.asarray(2 * PATCH * index + PATCH, F32)


def patch_at(r, c):
    return pl.ds(r * PATCH, PATCH), pl.ds(pl.multiple_of(c * PATCH, PATCH), PATCH)


def centres_of(columns):
    return [(centre_of(r), centre_of(c)) for r in range(2) for c in columns]


def eight(ref):
    return [ref.at[4 * edge + 2 * r + at] for r in range(2) for edge in range(2) for at in range(2)]


def own_kernel(odd_ref, own_ref, state_ref, part_ref, mean_ref, perturbation_ref):
    rows, cols, ensemble = state_ref.shape
    edge_columns, _ = sides(odd_ref[0], cols)
    part_ref[...] = jnp.zeros_like(part_ref)
    add_grams(eight(part_ref), own_ref[:, : own_ref.shape[1] // 2], (0.0, 0.0), centres_of(INNER + edge_columns))
    for r in range(rows // 8):
        at = slice(r * 8, (r + 1) * 8)
        mean, perturbation = centred(state_ref[at].reshape(8 * cols, ensemble))
        mean_ref[at] = mean.reshape(8, cols, ensemble)
        perturbation_ref[at] = perturbation.reshape(8, cols, ensemble)


def analyse(mean_ref, perturbation_ref, at, across, transform):
    ensemble = transform.shape[0]
    cells = perturbation_ref[at, across, :].reshape(PATCH * PATCH, ensemble)
    change = jnp.dot(cells, transform, preferred_element_type=F32)
    return (mean_ref[at, across, :] + change.reshape(PATCH, PATCH, ensemble)).astype(BF16)


def mid_kernel(odd_ref, column_ref, part_ref, mean_ref, perturbation_ref, out_ref, edge_ref, gram, half, z, right, transform):
    rows, cols, ensemble = mean_ref.shape
    edge_columns, _ = sides(odd_ref[0], cols)
    gram[...] = part_ref[:4]
    edge_ref[...] = part_ref[4:]
    refs = [ref.at[2 * r + at] for r in range(2) for ref in (gram, edge_ref) for at in range(2)]
    add_column(refs, column_ref, 0.0, centres_of(INNER + edge_columns), float(rows), own=False)
    solve(gram, half, z, right, transform, ensemble)
    for p in range(4):
        at, across = patch_at(p // 2, INNER[p % 2])
        out = analyse(mean_ref, perturbation_ref, at, across, transform[p])
        out_ref[at, pl.ds((p % 2) * PATCH, PATCH), :] = out


def edge_kernel(
    odd_ref, far_ref, near_ref, edge_ref, mean_ref, perturbation_ref, mid_ref, out_ref, gram, half, z, right, transform, done, semaphores
):
    rows, cols, ensemble = mean_ref.shape
    inner = pltpu.make_async_copy(mid_ref, out_ref.at[:, PATCH : cols - PATCH, :], semaphores.at[4])
    inner.start()
    edge_columns, shift = sides(odd_ref[0], cols)
    gram[...] = edge_ref[...]
    for at, (ref, col_shift) in enumerate(((near_ref, shift), (far_ref, -shift))):
        refs = [gram.at[at], gram.at[2 + at]]
        add_column(refs, ref, col_shift, centres_of(edge_columns[at : at + 1]), float(rows))
    solve(gram, half, z, right, transform, ensemble)
    copies = []
    for p in range(4):
        at, across = patch_at(p // 2, edge_columns[p % 2])
        done[p] = analyse(mean_ref, perturbation_ref, at, across, transform[p])
        copies.append(pltpu.make_async_copy(done.at[p], out_ref.at[at, across, :], semaphores.at[p]))
        copies[p].start()
    for copy in (inner, *copies):
        copy.wait()


def vmem(count):
    return [pl.BlockSpec(memory_space=pltpu.VMEM)] * count


SMEM = pl.BlockSpec(memory_space=pltpu.SMEM)


def scratch(ensemble):
    return [
        pltpu.VMEM((4, ensemble, ensemble + EXTRA), F32),
        pltpu.VMEM((4, ensemble, ensemble), F32),
        pltpu.VMEM((4, ensemble, ensemble), F32),
        pltpu.VMEM((4, ensemble, 2 * ensemble), BF16),
        pltpu.VMEM((4, ensemble, ensemble), BF16),
    ]


def pack(members, values, precision, cells, counts, tile_cols):
    capacity, ensemble = members.shape
    given = [pltpu.with_memory_space_constraint(x, pltpu.HBM) for x in (members, values, precision, cells)]
    return pl.pallas_call(
        functools.partial(pack_kernel, tile_cols=tile_cols),
        out_shape=pltpu.VMEM((ensemble + EXTRA, capacity), BF16),
        in_specs=[SMEM] + [pl.BlockSpec(memory_space=pltpu.HBM)] * len(given),
        out_specs=pl.BlockSpec(memory_space=pltpu.VMEM),
        scratch_shapes=[pltpu.VMEM(x.shape, x.dtype) for x in given] + [pltpu.SemaphoreType.DMA((len(given),))],
        compiler_params=pltpu.CompilerParams(vmem_limit_bytes=4 << 20),
    )(counts, *given)


def stack_kernel(own_ref, north_ref, south_ref, out_ref, *, tile_rows):
    rows, capacity = own_ref.shape
    kept = capacity // 2
    ensemble = rows - EXTRA
    tiles = (own_ref, north_ref, south_ref)
    for at, ref in enumerate(tiles):
        out_ref[at * rows : (at + 1) * rows, :] = ref[:, :kept]
    full = [
        jnp.max(ref[ensemble:, kept:].astype(F32)[WEIGHT : WEIGHT + 1], axis=1, keepdims=True) > 0.0 for ref in tiles[:2]
    ]

    def chosen(own, north, south):
        return jnp.where(full[0], own, jnp.where(full[1], north, south))

    spreads = [ref[:ensemble, kept:].astype(F32) for ref in tiles]
    scalars = [ref[ensemble:, kept:].astype(F32) for ref in tiles]
    index = lax.broadcasted_iota(jnp.int32, (EXTRA, kept), 0)
    shift = chosen(0.0, -float(tile_rows), float(tile_rows))
    out_ref[3 * rows : 3 * rows + ensemble, :] = chosen(*spreads).astype(BF16)
    out_ref[3 * rows + ensemble :, :] = (chosen(*scalars) + jnp.where(index == ROW, shift, 0.0)).astype(BF16)


def stack(own, north, south, tile_rows):
    rows, capacity = own.shape
    return pl.pallas_call(
        functools.partial(stack_kernel, tile_rows=tile_rows),
        out_shape=pltpu.VMEM((BLOCKS * rows, capacity // 2), BF16),
        in_specs=vmem(3),
        out_specs=pl.BlockSpec(memory_space=pltpu.VMEM),
        compiler_params=pltpu.CompilerParams(vmem_limit_bytes=4 << 20),
    )(own, north, south)


def own_part(odd, own, state):
    rows, cols, ensemble = state.shape
    return pl.pallas_call(
        own_kernel,
        out_shape=(
            pltpu.VMEM((8, ensemble, ensemble + EXTRA), F32),
            pltpu.VMEM(state.shape, F32),
            pltpu.VMEM(state.shape, BF16),
        ),
        in_specs=[SMEM] + vmem(2),
        out_specs=tuple(vmem(3)),
        compiler_params=pltpu.CompilerParams(vmem_limit_bytes=12 << 20),
        cost_estimate=pl.CostEstimate(flops=1 << 30, bytes_accessed=1 << 20, transcendentals=0),
    )(odd, own, state)


def middle(odd, column, part, mean, perturbation):
    rows, cols, ensemble = mean.shape
    return pl.pallas_call(
        mid_kernel,
        out_shape=(
            pltpu.VMEM((rows, cols - 2 * PATCH, ensemble), BF16),
            pltpu.VMEM((4, ensemble, ensemble + EXTRA), F32),
        ),
        in_specs=[SMEM] + vmem(4),
        out_specs=tuple(vmem(2)),
        scratch_shapes=scratch(ensemble),
        compiler_params=pltpu.CompilerParams(vmem_limit_bytes=12 << 20),
        cost_estimate=pl.CostEstimate(flops=1 << 32, bytes_accessed=1 << 20, transcendentals=0),
    )(odd, column, part, mean, perturbation)


def edges(odd, near, far, edge, mean, perturbation, mid):
    ensemble = mean.shape[-1]
    return pl.pallas_call(
        edge_kernel,
        out_shape=jax.ShapeDtypeStruct(mean.shape, BF16),
        in_specs=[SMEM] + vmem(6),
        out_specs=pl.BlockSpec(memory_space=pltpu.HBM),
        scratch_shapes=scratch(ensemble)
        + [pltpu.VMEM((4, PATCH, PATCH, ensemble), BF16), pltpu.SemaphoreType.DMA((5,))],
        compiler_params=pltpu.CompilerParams(vmem_limit_bytes=12 << 20),
    )(odd, far, near, edge, mean, perturbation, mid)


def shifted(x, axis, step):
    count = lax.axis_size(axis)
    return lax.ppermute(x, axis, [(i, i + step) for i in range(count) if 0 <= i + step < count])


def exchange(x, axis, first):
    count = lax.axis_size(axis)
    pairs = []
    for low in range(first, count, 2):
        high = (low + 1) % count
        pairs += [(low, high), (high, low)]
    return lax.ppermute(x, axis, pairs)


def body(state, obs_members, obs_values, obs_precision, obs_cells, obs_counts):
    _, tile_rows, tile_cols, ensemble = state.shape
    capacity = obs_members.shape[2]
    odd = (lax.axis_index("lon") & 1).astype(jnp.int32).reshape(1)
    own = pack(
        obs_members.reshape(capacity, ensemble),
        obs_values.reshape(1, capacity),
        obs_precision.reshape(1, capacity),
        obs_cells.reshape(1, capacity),
        obs_counts,
        tile_cols,
    )
    north = shifted(own, "lat", 1)
    south = shifted(own, "lat", -1)
    column = stack(own, north, south, tile_rows)
    far = exchange(column, "lon", 1)
    near = exchange(column, "lon", 0)
    part, mean, perturbation = own_part(odd, own, state.reshape(tile_rows, tile_cols, ensemble))
    mid, edge = middle(odd, column, part, mean, perturbation)
    out = edges(odd, near, far, edge, mean, perturbation, mid)
    return out.reshape(state.shape)


def solution(mesh):
    in_specs = (
        P(None, "lat", "lon", None),
        P("lat", "lon", None, None),
        P("lat", "lon", None),
        P("lat", "lon", None),
        P("lat", "lon", None),
        P("lat", "lon"),
    )
    out_specs = P(None, "lat", "lon", None)
    return jax.shard_map(body, mesh=mesh, in_specs=in_specs, out_specs=out_specs, check_vma=False)
```

```python
import functools

import jax
import jax.numpy as jnp
from jax import lax
from jax.experimental import pallas as pl
from jax.experimental.pallas import tpu as pltpu
from jax.sharding import PartitionSpec as P

PATCH = 16
NS_STEPS = 12
RAD = 24
EXTRA = 16
WEIGHT, ROW, COL = 2, 5, 6
UNROLL = 10
INNER = (1, 2)
BLOCKS = 4
F32, BF16 = jnp.float32, jnp.bfloat16


def halves(x):
    high = x.astype(BF16)
    return high, (x - high.astype(F32)).astype(BF16)


def thirds(x):
    high = x.astype(BF16)
    return high, *halves(x - high.astype(F32))


def side_by_side(x):
    return jnp.concatenate(halves(x), axis=1)


def pack_kernel(count_ref, members_in, values_in, precision_in, cells_in, out_ref, *scratch, tile_cols):
    *held, semaphores = scratch
    given = (members_in, values_in, precision_in, cells_in)
    copies = [pltpu.make_async_copy(a, b, semaphores.at[at]) for at, (a, b) in enumerate(zip(given, held))]
    for copy in copies:
        copy.start()
    for copy in copies:
        copy.wait()
    members_ref, values_ref, precision_ref, cells_ref = held
    capacity, ensemble = members_ref.shape
    members = members_ref[...].T.astype(F32)
    mean = jnp.sum(members, axis=0, keepdims=True) * (1.0 / ensemble)
    out_ref[:ensemble, :] = (members - mean).astype(BF16)
    slot = lax.broadcasted_iota(jnp.int32, (1, capacity), 1)
    weight = jnp.where(slot < count_ref[0, 0], precision_ref[...], 0.0)
    cells = cells_ref[...]
    rows = [
        *halves(values_ref[...] - mean),
        *thirds(weight),
        (cells // tile_cols).astype(BF16),
        (cells % tile_cols).astype(BF16),
    ]
    index = lax.broadcasted_iota(jnp.int32, (EXTRA, capacity), 0)
    extra = jnp.zeros((EXTRA, capacity), F32)
    for at, row in enumerate(rows):
        extra = jnp.where(index == at, row.astype(F32), extra)
    out_ref[ensemble:, :] = extra.astype(BF16)


def locals_of(scalars, row_shift, col_shift, centres):
    high, middle, low = (scalars[WEIGHT + at : WEIGHT + at + 1] for at in range(3))
    weight = high + (middle + low)
    rows_twice = 2.0 * (scalars[ROW : ROW + 1] + row_shift) + 1.0
    cols_twice = 2.0 * (scalars[COL : COL + 1] + col_shift) + 1.0
    count = len(centres)
    index = lax.broadcasted_iota(jnp.int32, (8, 1), 0)
    row_centre = jnp.zeros((8, 1), F32)
    col_centre = jnp.zeros((8, 1), F32)
    for at, (row, col) in enumerate(centres):
        row_centre = jnp.where(index == at, row, row_centre)
        col_centre = jnp.where(index == at, col, col_centre)
    row_gap = rows_twice - row_centre
    col_gap = cols_twice - col_centre
    distance = row_gap * row_gap + col_gap * col_gap
    taper = jnp.where(distance < 4.0 * RAD * RAD, jnp.exp(-distance / (2.0 * RAD * RAD)), 0.0)
    local = weight * taper
    return [local[at : at + 1] for at in range(count)]


def add_grams(gram_refs, payload, shifts, centres):
    ensemble = payload.shape[0] - EXTRA
    spread = payload[:ensemble].astype(F32)
    local = locals_of(payload[ensemble:].astype(F32), *shifts, centres)
    weighted = jnp.concatenate([(row * spread).astype(BF16) for row in local], axis=0)
    part = lax.dot_general(weighted, payload, (((1,), (1,)), ((), ())), preferred_element_type=F32)
    for at, ref in enumerate(gram_refs):
        ref[...] += part[at * ensemble : (at + 1) * ensemble]


def add_column(gram_refs, column_ref, col_shift, centres, tile_rows, own=True):
    payload = column_ref.shape[0] // BLOCKS
    half = len(gram_refs) // 2
    upper, lower = slice(0, half), slice(half, None)
    blocks = [column_ref[at * payload : (at + 1) * payload, :] for at in range(BLOCKS)]
    if own:
        add_grams(gram_refs, blocks[0], (0.0, col_shift), centres)
    add_grams(gram_refs[upper], blocks[1], (-tile_rows, col_shift), centres[upper])
    add_grams(gram_refs[lower], blocks[2], (tile_rows, col_shift), centres[lower])
    add_grams(gram_refs, blocks[3], (0.0, col_shift), centres)


def double_dot(left, right):
    width = right.shape[1] // 2
    both = jnp.dot(left, jnp.concatenate([right, right], axis=0), preferred_element_type=F32)
    return both[:, :width] + both[:, width:]


def solve(gram_ref, half_ref, z_ref, right_ref, transform_ref, ensemble):
    patches = range(gram_ref.shape[0])
    row = lax.broadcasted_iota(jnp.int32, (ensemble, ensemble), 0)
    col = lax.broadcasted_iota(jnp.int32, (ensemble, ensemble), 1)
    diagonal = row == col
    traces = []
    for p in patches:
        system = gram_ref[p, :, :ensemble] + jnp.where(diagonal, ensemble - 1.0, 0.0)
        on = jnp.where(diagonal, system, 0.0)
        trace = jnp.sum(jnp.sum(on, axis=0, keepdims=True), axis=1, keepdims=True)
        traces.append(trace)
        half = system * (-0.5 / trace)
        half_ref[p] = half
        right_ref[p] = side_by_side(half)
        z_ref[p] = jnp.where(diagonal, 1.5, 0.0) + half

    def times(matrix, column):
        across = jnp.sum(jnp.where(diagonal, column, 0.0), axis=0, keepdims=True)
        return jnp.sum(matrix * across, axis=1, keepdims=True)

    def first(p, with_root):
        right = right_ref[p]
        if with_root:
            z = z_ref[p]
            both = double_dot(jnp.concatenate([right, side_by_side(z)], axis=0), right)
            z_ref[p] = 1.5 * z + both[ensemble:]
        else:
            both = double_dot(right, right)
        half_ref[p] = 1.5 * half_ref[p] + both[:ensemble]

    def second(p):
        middle = half_ref[p]
        half = 1.5 * middle + double_dot(side_by_side(middle), right_ref[p])
        half_ref[p] = half
        right_ref[p] = side_by_side(half)

    def advance(with_root):
        split = len(patches) // 2
        for p in patches[:split]:
            first(p, with_root)
        for p in patches[split:]:
            first(p, with_root)
            second(p - split)
        for p in patches[split:]:
            second(p)

    def step(_, carry):
        advance(True)
        return carry

    advance(False)
    lax.fori_loop(0, NS_STEPS - 2, step, 0, unroll=UNROLL)
    for p in patches:
        z = z_ref[p]
        z_ref[p] = 1.5 * z + double_dot(side_by_side(z), right_ref[p])
    pulls = [gram_ref[p, :, ensemble : ensemble + 1] + gram_ref[p, :, ensemble + 1 : ensemble + 2] for p in patches]
    inner = [times(z_ref[p], pulls[p]) for p in patches]
    weights = [times(z_ref[p], inner[p]) for p in patches]
    for p in patches:
        scale = jnp.sqrt((ensemble - 1.0) / traces[p])
        transform_ref[p] = (z_ref[p] * scale + weights[p] / traces[p]).astype(BF16)


def centred(cells):
    ensemble = cells.shape[1]
    ones = jnp.full((ensemble, ensemble), 1.0 / ensemble, BF16)
    mean = jnp.dot(cells, ones, preferred_element_type=F32)
    return mean, (cells.astype(F32) - mean).astype(BF16)


def sides(odd, cols):
    last = cols // PATCH - 1
    shift = (1 - 2 * odd).astype(F32) * cols
    return (last * (1 - odd), last * odd), shift


def centre_of(index):
    return jnp.asarray(2 * PATCH * index + PATCH, F32)


def patch_at(r, c):
    return pl.ds(r * PATCH, PATCH), pl.ds(pl.multiple_of(c * PATCH, PATCH), PATCH)


def centres_of(columns):
    return [(centre_of(r), centre_of(c)) for r in range(2) for c in columns]


def eight(ref):
    return [ref.at[4 * edge + 2 * r + at] for r in range(2) for edge in range(2) for at in range(2)]


def own_kernel(odd_ref, own_ref, state_ref, part_ref, mean_ref, perturbation_ref):
    rows, cols, ensemble = state_ref.shape
    edge_columns, _ = sides(odd_ref[0], cols)
    part_ref[...] = jnp.zeros_like(part_ref)
    add_grams(eight(part_ref), own_ref[:, : own_ref.shape[1] // 2], (0.0, 0.0), centres_of(INNER + edge_columns))
    for r in range(rows // 8):
        at = slice(r * 8, (r + 1) * 8)
        mean, perturbation = centred(state_ref[at].reshape(8 * cols, ensemble))
        mean_ref[at] = mean.reshape(8, cols, ensemble)
        perturbation_ref[at] = perturbation.reshape(8, cols, ensemble)


def analyse(mean_ref, perturbation_ref, at, across, transform):
    ensemble = transform.shape[0]
    cells = perturbation_ref[at, across, :].reshape(PATCH * PATCH, ensemble)
    change = jnp.dot(cells, transform, preferred_element_type=F32)
    return (mean_ref[at, across, :] + change.reshape(PATCH, PATCH, ensemble)).astype(BF16)


def mid_kernel(odd_ref, column_ref, part_ref, mean_ref, perturbation_ref, out_ref, edge_ref, gram, half, z, right, transform):
    rows, cols, ensemble = mean_ref.shape
    edge_columns, _ = sides(odd_ref[0], cols)
    gram[...] = part_ref[:4]
    edge_ref[...] = part_ref[4:]
    refs = [ref.at[2 * r + at] for r in range(2) for ref in (gram, edge_ref) for at in range(2)]
    add_column(refs, column_ref, 0.0, centres_of(INNER + edge_columns), float(rows), own=False)
    solve(gram, half, z, right, transform, ensemble)
    for p in range(4):
        at, across = patch_at(p // 2, INNER[p % 2])
        out = analyse(mean_ref, perturbation_ref, at, across, transform[p])
        out_ref[at, pl.ds((p % 2) * PATCH, PATCH), :] = out


def edge_kernel(
    odd_ref, far_ref, near_ref, edge_ref, mean_ref, perturbation_ref, mid_ref, out_ref, gram, half, z, right, transform, done, semaphores
):
    rows, cols, ensemble = mean_ref.shape
    inner = pltpu.make_async_copy(mid_ref, out_ref.at[:, PATCH : cols - PATCH, :], semaphores.at[4])
    inner.start()
    edge_columns, shift = sides(odd_ref[0], cols)
    gram[...] = edge_ref[...]
    for at, (ref, col_shift) in enumerate(((near_ref, shift), (far_ref, -shift))):
        refs = [gram.at[at], gram.at[2 + at]]
        add_column(refs, ref, col_shift, centres_of(edge_columns[at : at + 1]), float(rows))
    solve(gram, half, z, right, transform, ensemble)
    copies = []
    for p in range(4):
        at, across = patch_at(p // 2, edge_columns[p % 2])
        done[p] = analyse(mean_ref, perturbation_ref, at, across, transform[p])
        copies.append(pltpu.make_async_copy(done.at[p], out_ref.at[at, across, :], semaphores.at[p]))
        copies[p].start()
    for copy in (inner, *copies):
        copy.wait()


def vmem(count):
    return [pl.BlockSpec(memory_space=pltpu.VMEM)] * count


SMEM = pl.BlockSpec(memory_space=pltpu.SMEM)


def scratch(ensemble):
    return [
        pltpu.VMEM((4, ensemble, ensemble + EXTRA), F32),
        pltpu.VMEM((4, ensemble, ensemble), F32),
        pltpu.VMEM((4, ensemble, ensemble), F32),
        pltpu.VMEM((4, ensemble, 2 * ensemble), BF16),
        pltpu.VMEM((4, ensemble, ensemble), BF16),
    ]


def pack(members, values, precision, cells, counts, tile_cols):
    capacity, ensemble = members.shape
    given = [pltpu.with_memory_space_constraint(x, pltpu.HBM) for x in (members, values, precision, cells)]
    return pl.pallas_call(
        functools.partial(pack_kernel, tile_cols=tile_cols),
        out_shape=pltpu.VMEM((ensemble + EXTRA, capacity), BF16),
        in_specs=[SMEM] + [pl.BlockSpec(memory_space=pltpu.HBM)] * len(given),
        out_specs=pl.BlockSpec(memory_space=pltpu.VMEM),
        scratch_shapes=[pltpu.VMEM(x.shape, x.dtype) for x in given] + [pltpu.SemaphoreType.DMA((len(given),))],
        compiler_params=pltpu.CompilerParams(vmem_limit_bytes=4 << 20),
    )(counts, *given)


def stack_kernel(own_ref, north_ref, south_ref, late_ref, out_ref, *, tile_rows):
    rows, capacity = own_ref.shape
    kept = capacity // 2
    ensemble = rows - EXTRA
    tiles = (own_ref[...], north_ref[...] + late_ref[...], south_ref[...])
    for at, tile in enumerate(tiles):
        out_ref[at * rows : (at + 1) * rows, :] = tile[:, :kept]
    full = [
        jnp.max(tile[ensemble:, kept:].astype(F32)[WEIGHT : WEIGHT + 1], axis=1, keepdims=True) > 0.0 for tile in tiles[:2]
    ]

    def chosen(own, north, south):
        return jnp.where(full[0], own, jnp.where(full[1], north, south))

    spreads = [tile[:ensemble, kept:].astype(F32) for tile in tiles]
    scalars = [tile[ensemble:, kept:].astype(F32) for tile in tiles]
    index = lax.broadcasted_iota(jnp.int32, (EXTRA, kept), 0)
    shift = chosen(0.0, -float(tile_rows), float(tile_rows))
    out_ref[3 * rows : 3 * rows + ensemble, :] = chosen(*spreads).astype(BF16)
    out_ref[3 * rows + ensemble :, :] = (chosen(*scalars) + jnp.where(index == ROW, shift, 0.0)).astype(BF16)


def stack(own, north, south, late, tile_rows):
    rows, capacity = own.shape
    return pl.pallas_call(
        functools.partial(stack_kernel, tile_rows=tile_rows),
        out_shape=pltpu.VMEM((BLOCKS * rows, capacity // 2), BF16),
        in_specs=vmem(4),
        out_specs=pl.BlockSpec(memory_space=pltpu.VMEM),
        compiler_params=pltpu.CompilerParams(vmem_limit_bytes=4 << 20),
    )(own, north, south, late)


def own_part(odd, own, state):
    rows, cols, ensemble = state.shape
    return pl.pallas_call(
        own_kernel,
        out_shape=(
            pltpu.VMEM((8, ensemble, ensemble + EXTRA), F32),
            pltpu.VMEM(state.shape, F32),
            pltpu.VMEM(state.shape, BF16),
        ),
        in_specs=[SMEM] + vmem(2),
        out_specs=tuple(vmem(3)),
        compiler_params=pltpu.CompilerParams(vmem_limit_bytes=12 << 20),
        cost_estimate=pl.CostEstimate(flops=1 << 30, bytes_accessed=1 << 20, transcendentals=0),
    )(odd, own, state)


def middle(odd, column, part, mean, perturbation):
    rows, cols, ensemble = mean.shape
    return pl.pallas_call(
        mid_kernel,
        out_shape=(
            pltpu.VMEM((rows, cols - 2 * PATCH, ensemble), BF16),
            pltpu.VMEM((4, ensemble, ensemble + EXTRA), F32),
        ),
        in_specs=[SMEM] + vmem(4),
        out_specs=tuple(vmem(2)),
        scratch_shapes=scratch(ensemble),
        compiler_params=pltpu.CompilerParams(vmem_limit_bytes=12 << 20),
        cost_estimate=pl.CostEstimate(flops=1 << 32, bytes_accessed=1 << 20, transcendentals=0),
    )(odd, column, part, mean, perturbation)


def edges(odd, near, far, edge, mean, perturbation, mid):
    ensemble = mean.shape[-1]
    return pl.pallas_call(
        edge_kernel,
        out_shape=jax.ShapeDtypeStruct(mean.shape, BF16),
        in_specs=[SMEM] + vmem(6),
        out_specs=pl.BlockSpec(memory_space=pltpu.HBM),
        scratch_shapes=scratch(ensemble)
        + [pltpu.VMEM((4, PATCH, PATCH, ensemble), BF16), pltpu.SemaphoreType.DMA((5,))],
        compiler_params=pltpu.CompilerParams(vmem_limit_bytes=12 << 20),
    )(odd, far, near, edge, mean, perturbation, mid)


def shifts(x):
    count = lax.axis_size("lat")
    upper = count // 2 - 1
    southward = [(i, i + 1) for i in range(count - 1) if i + 1 != upper]
    northward = [(i + 1, i) for i in range(count - 1)]
    return [lax.ppermute(x, "lat", pairs) for pairs in (southward, northward, [(upper - 1, upper)])]


def exchange(x, axis, first):
    count = lax.axis_size(axis)
    pairs = []
    for low in range(first, count, 2):
        high = (low + 1) % count
        pairs += [(low, high), (high, low)]
    return lax.ppermute(x, axis, pairs)


def body(state, obs_members, obs_values, obs_precision, obs_cells, obs_counts):
    _, tile_rows, tile_cols, ensemble = state.shape
    capacity = obs_members.shape[2]
    odd = (lax.axis_index("lon") & 1).astype(jnp.int32).reshape(1)
    own = pack(
        obs_members.reshape(capacity, ensemble),
        obs_values.reshape(1, capacity),
        obs_precision.reshape(1, capacity),
        obs_cells.reshape(1, capacity),
        obs_counts,
        tile_cols,
    )
    column = stack(own, *shifts(own), tile_rows)
    far = exchange(column, "lon", 1)
    near = exchange(column, "lon", 0)
    part, mean, perturbation = own_part(odd, own, state.reshape(tile_rows, tile_cols, ensemble))
    mid, edge = middle(odd, column, part, mean, perturbation)
    out = edges(odd, near, far, edge, mean, perturbation, mid)
    return out.reshape(state.shape)


def solution(mesh):
    in_specs = (
        P(None, "lat", "lon", None),
        P("lat", "lon", None, None),
        P("lat", "lon", None),
        P("lat", "lon", None),
        P("lat", "lon", None),
        P("lat", "lon"),
    )
    out_specs = P(None, "lat", "lon", None)
    return jax.shard_map(body, mesh=mesh, in_specs=in_specs, out_specs=out_specs, check_vma=False)
```

```python
import functools
from typing import Any, NamedTuple

import jax
import jax.numpy as jnp
from jax import lax
from jax.experimental import pallas as pl
from jax.experimental.pallas import tpu as pltpu
from jax.sharding import PartitionSpec as P

PATCH = 16
NS_STEPS = 12
RAD = 24
EXTRA = 16
WEIGHT, ROW, COL = 2, 5, 6
EARLY_STEPS = 7
INNER = (1, 2)
BLOCKS = 4
F32, BF16 = jnp.float32, jnp.bfloat16


def halves(x):
    high = x.astype(BF16)
    return high, (x - high.astype(F32)).astype(BF16)


def thirds(x):
    high = x.astype(BF16)
    return high, *halves(x - high.astype(F32))


def side_by_side(x):
    return jnp.concatenate(halves(x), axis=1)


def pack_kernel(count_ref, members_in, values_in, precision_in, cells_in, out_ref, *scratch, tile_cols):
    *held, semaphores = scratch
    given = (members_in, values_in, precision_in, cells_in)
    copies = [pltpu.make_async_copy(a, b, semaphores.at[at]) for at, (a, b) in enumerate(zip(given, held))]
    for copy in copies:
        copy.start()
    for copy in copies:
        copy.wait()
    members_ref, values_ref, precision_ref, cells_ref = held
    capacity, ensemble = members_ref.shape
    members = members_ref[...].T.astype(F32)
    mean = jnp.sum(members, axis=0, keepdims=True) * (1.0 / ensemble)
    out_ref[:ensemble, :] = (members - mean).astype(BF16)
    slot = lax.broadcasted_iota(jnp.int32, (1, capacity), 1)
    weight = jnp.where(slot < count_ref[0, 0], precision_ref[...], 0.0)
    cells = cells_ref[...]
    rows = [
        *halves(values_ref[...] - mean),
        *thirds(weight),
        (cells // tile_cols).astype(BF16),
        (cells % tile_cols).astype(BF16),
    ]
    index = lax.broadcasted_iota(jnp.int32, (EXTRA, capacity), 0)
    extra = jnp.zeros((EXTRA, capacity), F32)
    for at, row in enumerate(rows):
        extra = jnp.where(index == at, row.astype(F32), extra)
    out_ref[ensemble:, :] = extra.astype(BF16)


def locals_of(scalars, row_shift, col_shift, centres):
    high, middle, low = (scalars[WEIGHT + at : WEIGHT + at + 1] for at in range(3))
    weight = high + (middle + low)
    rows_twice = 2.0 * (scalars[ROW : ROW + 1] + row_shift) + 1.0
    cols_twice = 2.0 * (scalars[COL : COL + 1] + col_shift) + 1.0
    count = len(centres)
    index = lax.broadcasted_iota(jnp.int32, (8, 1), 0)
    row_centre = jnp.zeros((8, 1), F32)
    col_centre = jnp.zeros((8, 1), F32)
    for at, (row, col) in enumerate(centres):
        row_centre = jnp.where(index == at, row, row_centre)
        col_centre = jnp.where(index == at, col, col_centre)
    row_gap = rows_twice - row_centre
    col_gap = cols_twice - col_centre
    distance = row_gap * row_gap + col_gap * col_gap
    taper = jnp.where(distance < 4.0 * RAD * RAD, jnp.exp(-distance / (2.0 * RAD * RAD)), 0.0)
    local = weight * taper
    return [local[at : at + 1] for at in range(count)]


def add_grams(gram_refs, payload, shifts, centres):
    ensemble = payload.shape[0] - EXTRA
    spread = payload[:ensemble].astype(F32)
    local = locals_of(payload[ensemble:].astype(F32), *shifts, centres)
    weighted = jnp.concatenate([(row * spread).astype(BF16) for row in local], axis=0)
    part = lax.dot_general(weighted, payload, (((1,), (1,)), ((), ())), preferred_element_type=F32)
    for at, ref in enumerate(gram_refs):
        ref[...] += part[at * ensemble : (at + 1) * ensemble]


def add_column(gram_refs, column_ref, col_shift, centres, tile_rows, own=True):
    payload = column_ref.shape[0] // BLOCKS
    half = len(gram_refs) // 2
    upper, lower = slice(0, half), slice(half, None)
    blocks = [column_ref[at * payload : (at + 1) * payload, :] for at in range(BLOCKS)]
    if own:
        add_grams(gram_refs, blocks[0], (0.0, col_shift), centres)
    add_grams(gram_refs[upper], blocks[1], (-tile_rows, col_shift), centres[upper])
    add_grams(gram_refs[lower], blocks[2], (tile_rows, col_shift), centres[lower])
    add_grams(gram_refs, blocks[3], (0.0, col_shift), centres)


def double_dot(left, right):
    width = right.shape[1] // 2
    both = jnp.dot(left, jnp.concatenate([right, right], axis=0), preferred_element_type=F32)
    return both[:, :width] + both[:, width:]


class Patch(NamedTuple):
    gram: Any
    half: Any
    z: Any
    right: Any


def patches_of(gram, half, z, right):
    return [Patch(gram.at[p], half.at[p], z.at[p], right.at[p]) for p in range(half.shape[0])]


def diagonal_of(ensemble):
    row = lax.broadcasted_iota(jnp.int32, (ensemble, ensemble), 0)
    return row == lax.broadcasted_iota(jnp.int32, (ensemble, ensemble), 1)


def system_of(patch):
    ensemble = patch.half.shape[0]
    diagonal = diagonal_of(ensemble)
    system = patch.gram[:, :ensemble] + jnp.where(diagonal, ensemble - 1.0, 0.0)
    on = jnp.where(diagonal, system, 0.0)
    return system, jnp.sum(jnp.sum(on, axis=0, keepdims=True), axis=1, keepdims=True)


def begin(patch):
    system, trace = system_of(patch)
    half = system * (-0.5 / trace)
    patch.half[...] = half
    patch.right[...] = side_by_side(half)
    patch.z[...] = jnp.where(diagonal_of(half.shape[0]), 1.5, 0.0) + half


def first(patch, with_root):
    right = patch.right[...]
    ensemble = right.shape[0]
    if with_root:
        z = patch.z[...]
        both = double_dot(jnp.concatenate([right, side_by_side(z)], axis=0), right)
        patch.z[...] = 1.5 * z + both[ensemble:]
    else:
        both = double_dot(right, right)
    patch.half[...] = 1.5 * patch.half[...] + both[:ensemble]


def second(patch):
    middle = patch.half[...]
    half = 1.5 * middle + double_dot(side_by_side(middle), patch.right[...])
    patch.half[...] = half
    patch.right[...] = side_by_side(half)


def advance(some, others, with_root=(True, True)):
    for p in some:
        first(p, with_root[0])
    for at in range(max(len(some), len(others))):
        if at < len(others):
            first(others[at], with_root[1])
        if at < len(some):
            second(some[at])
    for p in others:
        second(p)


def finish(patches):
    for p in patches:
        z = p.z[...]
        p.z[...] = 1.5 * z + double_dot(side_by_side(z), p.right[...])
    ensemble = patches[0].half.shape[0]
    diagonal = diagonal_of(ensemble)

    def times(matrix, column):
        across = jnp.sum(jnp.where(diagonal, column, 0.0), axis=0, keepdims=True)
        return jnp.sum(matrix * across, axis=1, keepdims=True)

    pulls = [p.gram[:, ensemble : ensemble + 1] + p.gram[:, ensemble + 1 : ensemble + 2] for p in patches]
    inner = [times(p.z[...], pull) for p, pull in zip(patches, pulls)]
    weights = [times(p.z[...], column) for p, column in zip(patches, inner)]
    traces = [system_of(p)[1] for p in patches]
    return [
        (p.z[...] * jnp.sqrt((ensemble - 1.0) / trace) + weight / trace).astype(BF16)
        for p, trace, weight in zip(patches, traces, weights)
    ]


def centred(cells):
    ensemble = cells.shape[1]
    ones = jnp.full((ensemble, ensemble), 1.0 / ensemble, BF16)
    mean = jnp.dot(cells, ones, preferred_element_type=F32)
    return mean, (cells.astype(F32) - mean).astype(BF16)


def sides(odd, cols):
    last = cols // PATCH - 1
    shift = (1 - 2 * odd).astype(F32) * cols
    return (last * (1 - odd), last * odd), shift


def centre_of(index):
    return jnp.asarray(2 * PATCH * index + PATCH, F32)


def patch_at(r, c):
    return pl.ds(r * PATCH, PATCH), pl.ds(pl.multiple_of(c * PATCH, PATCH), PATCH)


def centres_of(columns):
    return [(centre_of(r), centre_of(c)) for r in range(2) for c in columns]


def eight(ref):
    return [ref.at[4 * edge + 2 * r + at] for r in range(2) for edge in range(2) for at in range(2)]


def own_kernel(odd_ref, own_ref, state_ref, part_ref, mean_ref, perturbation_ref):
    rows, cols, ensemble = state_ref.shape
    edge_columns, _ = sides(odd_ref[0], cols)
    part_ref[...] = jnp.zeros_like(part_ref)
    add_grams(eight(part_ref), own_ref[:, : own_ref.shape[1] // 2], (0.0, 0.0), centres_of(INNER + edge_columns))
    for r in range(rows // 8):
        at = slice(r * 8, (r + 1) * 8)
        mean, perturbation = centred(state_ref[at].reshape(8 * cols, ensemble))
        mean_ref[at] = mean.reshape(8, cols, ensemble)
        perturbation_ref[at] = perturbation.reshape(8, cols, ensemble)


def analyse(mean_ref, perturbation_ref, at, across, transform):
    ensemble = transform.shape[0]
    cells = perturbation_ref[at, across, :].reshape(PATCH * PATCH, ensemble)
    change = jnp.dot(cells, transform, preferred_element_type=F32)
    return (mean_ref[at, across, :] + change.reshape(PATCH, PATCH, ensemble)).astype(BF16)


def mid_kernel(odd_ref, column_ref, part_ref, gram, half, z, right, *, tile):
    edge_columns, _ = sides(odd_ref[0], tile[1])
    gram[...] = part_ref[...]
    add_column(eight(gram), column_ref, 0.0, centres_of(INNER + edge_columns), float(tile[0]), own=False)
    inner = patches_of(gram, half, z, right)
    for p in inner:
        begin(p)
    advance(inner[:2], inner[2:], (False, False))
    for _ in range(EARLY_STEPS):
        advance(inner[:2], inner[2:])


def edge_kernel(
    odd_ref, far_ref, near_ref, gram_ref, half_ref, z_ref, mean_ref, perturbation_ref, out_ref, gram, half, z, right, done, semaphores
):
    rows, cols, ensemble = mean_ref.shape
    edge_columns, shift = sides(odd_ref[0], cols)
    gram[...] = gram_ref[...]
    half[:4] = half_ref[...]
    z[:4] = z_ref[...]
    patches = patches_of(gram, half, z, right)
    inner, edge = patches[:4], patches[4:]
    for p in inner:
        p.right[...] = side_by_side(p.half[...])
    for at, (ref, col_shift) in enumerate(((near_ref, shift), (far_ref, -shift))):
        refs = [edge[at].gram, edge[2 + at].gram]
        add_column(refs, ref, col_shift, centres_of(edge_columns[at : at + 1]), float(rows))
    for p in edge:
        begin(p)

    copies = []

    def put(transforms, columns):
        for p, transform in enumerate(transforms):
            at, across = patch_at(p // 2, columns[p % 2])
            slot = len(copies)
            done[slot] = analyse(mean_ref, perturbation_ref, at, across, transform)
            copies.append(pltpu.make_async_copy(done.at[slot], out_ref.at[at, across, :], semaphores.at[slot]))
            copies[slot].start()

    left = NS_STEPS - 2 - EARLY_STEPS
    for step in range(NS_STEPS - 1):
        with_root = step > 0
        if step < left:
            advance(inner, edge, (True, with_root))
        else:
            advance(edge[:2], edge[2:], (with_root, with_root))
        if step == left:
            put(finish(inner), INNER)
    put(finish(edge), edge_columns)
    for copy in copies:
        copy.wait()


def vmem(count):
    return [pl.BlockSpec(memory_space=pltpu.VMEM)] * count


SMEM = pl.BlockSpec(memory_space=pltpu.SMEM)


def pack(members, values, precision, cells, counts, tile_cols):
    capacity, ensemble = members.shape
    given = [pltpu.with_memory_space_constraint(x, pltpu.HBM) for x in (members, values, precision, cells)]
    return pl.pallas_call(
        functools.partial(pack_kernel, tile_cols=tile_cols),
        out_shape=pltpu.VMEM((ensemble + EXTRA, capacity), BF16),
        in_specs=[SMEM] + [pl.BlockSpec(memory_space=pltpu.HBM)] * len(given),
        out_specs=pl.BlockSpec(memory_space=pltpu.VMEM),
        scratch_shapes=[pltpu.VMEM(x.shape, x.dtype) for x in given] + [pltpu.SemaphoreType.DMA((len(given),))],
        compiler_params=pltpu.CompilerParams(vmem_limit_bytes=4 << 20),
    )(counts, *given)


def stack_kernel(own_ref, north_ref, south_ref, late_ref, out_ref, *, tile_rows):
    rows, capacity = own_ref.shape
    kept = capacity // 2
    ensemble = rows - EXTRA
    tiles = (own_ref[...], north_ref[...] + late_ref[...], south_ref[...])
    for at, tile in enumerate(tiles):
        out_ref[at * rows : (at + 1) * rows, :] = tile[:, :kept]
    full = [
        jnp.max(tile[ensemble:, kept:].astype(F32)[WEIGHT : WEIGHT + 1], axis=1, keepdims=True) > 0.0 for tile in tiles[:2]
    ]

    def chosen(own, north, south):
        return jnp.where(full[0], own, jnp.where(full[1], north, south))

    spreads = [tile[:ensemble, kept:].astype(F32) for tile in tiles]
    scalars = [tile[ensemble:, kept:].astype(F32) for tile in tiles]
    index = lax.broadcasted_iota(jnp.int32, (EXTRA, kept), 0)
    shift = chosen(0.0, -float(tile_rows), float(tile_rows))
    out_ref[3 * rows : 3 * rows + ensemble, :] = chosen(*spreads).astype(BF16)
    out_ref[3 * rows + ensemble :, :] = (chosen(*scalars) + jnp.where(index == ROW, shift, 0.0)).astype(BF16)


def stack(own, north, south, late, tile_rows):
    rows, capacity = own.shape
    return pl.pallas_call(
        functools.partial(stack_kernel, tile_rows=tile_rows),
        out_shape=pltpu.VMEM((BLOCKS * rows, capacity // 2), BF16),
        in_specs=vmem(4),
        out_specs=pl.BlockSpec(memory_space=pltpu.VMEM),
        compiler_params=pltpu.CompilerParams(vmem_limit_bytes=4 << 20),
    )(own, north, south, late)


def own_part(odd, own, state):
    rows, cols, ensemble = state.shape
    return pl.pallas_call(
        own_kernel,
        out_shape=(
            pltpu.VMEM((8, ensemble, ensemble + EXTRA), F32),
            pltpu.VMEM(state.shape, F32),
            pltpu.VMEM(state.shape, BF16),
        ),
        in_specs=[SMEM] + vmem(2),
        out_specs=tuple(vmem(3)),
        compiler_params=pltpu.CompilerParams(vmem_limit_bytes=12 << 20),
        cost_estimate=pl.CostEstimate(flops=1 << 30, bytes_accessed=1 << 20, transcendentals=0),
    )(odd, own, state)


def middle(odd, column, part, tile):
    ensemble = part.shape[1]
    return pl.pallas_call(
        functools.partial(mid_kernel, tile=tile),
        out_shape=(
            pltpu.VMEM(part.shape, F32),
            pltpu.VMEM((4, ensemble, ensemble), F32),
            pltpu.VMEM((4, ensemble, ensemble), F32),
        ),
        in_specs=[SMEM] + vmem(2),
        out_specs=tuple(vmem(3)),
        scratch_shapes=[pltpu.VMEM((4, ensemble, 2 * ensemble), BF16)],
        compiler_params=pltpu.CompilerParams(vmem_limit_bytes=12 << 20),
        cost_estimate=pl.CostEstimate(flops=1 << 32, bytes_accessed=1 << 20, transcendentals=0),
    )(odd, column, part)


def edges(odd, near, far, gram, half, z, mean, perturbation):
    ensemble = mean.shape[-1]
    return pl.pallas_call(
        edge_kernel,
        out_shape=jax.ShapeDtypeStruct(mean.shape, BF16),
        in_specs=[SMEM] + vmem(7),
        out_specs=pl.BlockSpec(memory_space=pltpu.HBM),
        scratch_shapes=[
            pltpu.VMEM(gram.shape, F32),
            pltpu.VMEM((8, ensemble, ensemble), F32),
            pltpu.VMEM((8, ensemble, ensemble), F32),
            pltpu.VMEM((8, ensemble, 2 * ensemble), BF16),
            pltpu.VMEM((8, PATCH, PATCH, ensemble), BF16),
            pltpu.SemaphoreType.DMA((8,)),
        ],
        compiler_params=pltpu.CompilerParams(vmem_limit_bytes=12 << 20),
    )(odd, far, near, gram, half, z, mean, perturbation)


def shifts(x):
    count = lax.axis_size("lat")
    upper = count // 2 - 1
    southward = [(i, i + 1) for i in range(count - 1) if i + 1 != upper]
    northward = [(i + 1, i) for i in range(count - 1)]
    return [lax.ppermute(x, "lat", pairs) for pairs in (southward, northward, [(upper - 1, upper)])]


def exchange(x, axis, first):
    count = lax.axis_size(axis)
    pairs = []
    for low in range(first, count, 2):
        high = (low + 1) % count
        pairs += [(low, high), (high, low)]
    return lax.ppermute(x, axis, pairs)


def body(state, obs_members, obs_values, obs_precision, obs_cells, obs_counts):
    _, tile_rows, tile_cols, ensemble = state.shape
    capacity = obs_members.shape[2]
    odd = (lax.axis_index("lon") & 1).astype(jnp.int32).reshape(1)
    own = pack(
        obs_members.reshape(capacity, ensemble),
        obs_values.reshape(1, capacity),
        obs_precision.reshape(1, capacity),
        obs_cells.reshape(1, capacity),
        obs_counts,
        tile_cols,
    )
    column = stack(own, *shifts(own), tile_rows)
    far = exchange(column, "lon", 1)
    near = exchange(column, "lon", 0)
    part, mean, perturbation = own_part(odd, own, state.reshape(tile_rows, tile_cols, ensemble))
    gram, half, z = middle(odd, column, part, (tile_rows, tile_cols))
    out = edges(odd, near, far, gram, half, z, mean, perturbation)
    return out.reshape(state.shape)


def solution(mesh):
    in_specs = (
        P(None, "lat", "lon", None),
        P("lat", "lon", None, None),
        P("lat", "lon", None),
        P("lat", "lon", None),
        P("lat", "lon", None),
        P("lat", "lon"),
    )
    out_specs = P(None, "lat", "lon", None)
    return jax.shard_map(body, mesh=mesh, in_specs=in_specs, out_specs=out_specs, check_vma=False)
```

```python
import functools
from typing import Any, NamedTuple

import jax
import jax.numpy as jnp
from jax import lax
from jax.experimental import pallas as pl
from jax.experimental.pallas import tpu as pltpu
from jax.sharding import PartitionSpec as P

PATCH = 16
NS_STEPS = 12
RAD = 24
EXTRA = 8
WEIGHT, ROW, COL = 2, 5, 6
EARLY_STEPS = 7
INNER = (1, 2)
BLOCKS = 4
F32, BF16 = jnp.float32, jnp.bfloat16


def halves(x):
    high = x.astype(BF16)
    return high, (x - high.astype(F32)).astype(BF16)


def thirds(x):
    high = x.astype(BF16)
    return high, *halves(x - high.astype(F32))


def side_by_side(x):
    return jnp.concatenate(halves(x), axis=1)


def pack_kernel(count_ref, members_in, values_in, precision_in, cells_in, out_ref, *scratch, tile_cols):
    *held, semaphores = scratch
    given = (members_in, values_in, precision_in, cells_in)
    copies = [pltpu.make_async_copy(a, b, semaphores.at[at]) for at, (a, b) in enumerate(zip(given, held))]
    for copy in copies:
        copy.start()
    for copy in copies:
        copy.wait()
    members_ref, values_ref, precision_ref, cells_ref = held
    capacity, ensemble = members_ref.shape
    members = members_ref[...].T.astype(F32)
    mean = jnp.sum(members, axis=0, keepdims=True) * (1.0 / ensemble)
    out_ref[:ensemble, :] = (members - mean).astype(BF16)
    slot = lax.broadcasted_iota(jnp.int32, (1, capacity), 1)
    weight = jnp.where(slot < count_ref[0, 0], precision_ref[...], 0.0)
    cells = cells_ref[...]
    rows = [
        *halves(values_ref[...] - mean),
        *thirds(weight),
        (cells // tile_cols).astype(BF16),
        (cells % tile_cols).astype(BF16),
    ]
    index = lax.broadcasted_iota(jnp.int32, (EXTRA, capacity), 0)
    extra = jnp.zeros((EXTRA, capacity), F32)
    for at, row in enumerate(rows):
        extra = jnp.where(index == at, row.astype(F32), extra)
    out_ref[ensemble:, :] = extra.astype(BF16)


def locals_of(scalars, row_shift, col_shift, centres):
    high, middle, low = (scalars[WEIGHT + at : WEIGHT + at + 1] for at in range(3))
    weight = high + (middle + low)
    rows_twice = 2.0 * (scalars[ROW : ROW + 1] + row_shift) + 1.0
    cols_twice = 2.0 * (scalars[COL : COL + 1] + col_shift) + 1.0
    count = len(centres)
    index = lax.broadcasted_iota(jnp.int32, (8, 1), 0)
    row_centre = jnp.zeros((8, 1), F32)
    col_centre = jnp.zeros((8, 1), F32)
    for at, (row, col) in enumerate(centres):
        row_centre = jnp.where(index == at, row, row_centre)
        col_centre = jnp.where(index == at, col, col_centre)
    row_gap = rows_twice - row_centre
    col_gap = cols_twice - col_centre
    distance = row_gap * row_gap + col_gap * col_gap
    taper = jnp.where(distance < 4.0 * RAD * RAD, jnp.exp(-distance / (2.0 * RAD * RAD)), 0.0)
    local = weight * taper
    return [local[at : at + 1] for at in range(count)]


def grams_of(blocks, shifts, centres):
    ensemble = blocks[0].shape[0] - EXTRA
    weighted = []
    for payload, shift in zip(blocks, shifts):
        spread = payload[:ensemble].astype(F32)
        local = locals_of(payload[ensemble:].astype(F32), *shift, centres)
        weighted.append(jnp.concatenate([(row * spread).astype(BF16) for row in local], axis=0))
    left, right = jnp.concatenate(weighted, axis=1), jnp.concatenate(blocks, axis=1)
    return lax.dot_general(left, right, (((1,), (1,)), ((), ())), preferred_element_type=F32)


def add_column(pairs, column_ref, col_shift, centres, tile_rows, own=True):
    ensemble = column_ref.shape[0] - EXTRA
    kept = column_ref.shape[1] // BLOCKS
    half = len(pairs) // 2
    blocks = [column_ref[:, at * kept : (at + 1) * kept] for at in range(BLOCKS)]
    for at, row_shift in ((0, -tile_rows), (1, tile_rows)):
        here = slice(at * half, (at + 1) * half)
        used = [(blocks[1 + at], row_shift), (blocks[3], 0.0)] + ([(blocks[0], 0.0)] if own else [])
        part = grams_of([block for block, _ in used], [(shift, col_shift) for _, shift in used], centres[here])
        for p, (given, out) in enumerate(pairs[here]):
            out[...] = given[...] + part[p * ensemble : (p + 1) * ensemble]


def double_dot(left, right):
    width = right.shape[1] // 2
    both = jnp.dot(left, jnp.concatenate([right, right], axis=0), preferred_element_type=F32)
    return both[:, :width] + both[:, width:]


class Patch(NamedTuple):
    gram: Any
    half: Any
    z: Any
    right: Any


def patches_of(gram, half, z, right):
    return [Patch(gram.at[p], half.at[p], z.at[p], right.at[p]) for p in range(half.shape[0])]


def diagonal_of(ensemble):
    row = lax.broadcasted_iota(jnp.int32, (ensemble, ensemble), 0)
    return row == lax.broadcasted_iota(jnp.int32, (ensemble, ensemble), 1)


def system_of(patch):
    ensemble = patch.half.shape[0]
    diagonal = diagonal_of(ensemble)
    system = patch.gram[:, :ensemble] + jnp.where(diagonal, ensemble - 1.0, 0.0)
    on = jnp.where(diagonal, system, 0.0)
    return system, jnp.sum(jnp.sum(on, axis=0, keepdims=True), axis=1, keepdims=True)


def begin(patch):
    system, trace = system_of(patch)
    half = system * (-0.5 / trace)
    patch.half[...] = half
    patch.right[...] = side_by_side(half)
    patch.z[...] = jnp.where(diagonal_of(half.shape[0]), 1.5, 0.0) + half
    return trace


def first(patch, with_root):
    right = patch.right[...]
    ensemble = right.shape[0]
    if with_root:
        z = patch.z[...]
        both = double_dot(jnp.concatenate([right, side_by_side(z)], axis=0), right)
        patch.z[...] = 1.5 * z + both[ensemble:]
    else:
        both = double_dot(right, right)
    patch.half[...] = 1.5 * patch.half[...] + both[:ensemble]


def second(patch):
    middle = patch.half[...]
    half = 1.5 * middle + double_dot(side_by_side(middle), patch.right[...])
    patch.half[...] = half
    patch.right[...] = side_by_side(half)


def advance(some, others, with_root=(True, True)):
    for p in some:
        first(p, with_root[0])
    for at in range(max(len(some), len(others))):
        if at < len(others):
            first(others[at], with_root[1])
        if at < len(some):
            second(some[at])
    for p in others:
        second(p)


def finish(patches, traces):
    for p in patches:
        z = p.z[...]
        p.z[...] = 1.5 * z + double_dot(side_by_side(z), p.right[...])
    ensemble = patches[0].half.shape[0]
    diagonal = diagonal_of(ensemble)

    def times(matrix, column):
        across = jnp.sum(jnp.where(diagonal, column, 0.0), axis=0, keepdims=True)
        return jnp.sum(matrix * across, axis=1, keepdims=True)

    pulls = [p.gram[:, ensemble : ensemble + 1] + p.gram[:, ensemble + 1 : ensemble + 2] for p in patches]
    inner = [times(p.z[...], pull) for p, pull in zip(patches, pulls)]
    weights = [times(p.z[...], column) for p, column in zip(patches, inner)]
    return [
        (p.z[...] * jnp.sqrt((ensemble - 1.0) / trace) + weight / trace).astype(BF16)
        for p, trace, weight in zip(patches, traces, weights)
    ]


def centred(cells):
    ensemble = cells.shape[1]
    ones = jnp.full((ensemble, ensemble), 1.0 / ensemble, BF16)
    mean = jnp.dot(cells, ones, preferred_element_type=F32)
    return mean, (cells.astype(F32) - mean).astype(BF16)


def sides(odd, cols):
    last = cols // PATCH - 1
    shift = (1 - 2 * odd).astype(F32) * cols
    return (last * (1 - odd), last * odd), shift


def centre_of(index):
    return jnp.asarray(2 * PATCH * index + PATCH, F32)


def patch_at(r, c):
    return pl.ds(r * PATCH, PATCH), pl.ds(pl.multiple_of(c * PATCH, PATCH), PATCH)


def centres_of(columns):
    return [(centre_of(r), centre_of(c)) for r in range(2) for c in columns]


def eight(ref):
    return [ref.at[4 * edge + 2 * r + at] for r in range(2) for edge in range(2) for at in range(2)]


def own_kernel(odd_ref, own_ref, state_ref, part_ref, mean_ref, perturbation_ref):
    rows, cols, ensemble = state_ref.shape
    edge_columns, _ = sides(odd_ref[0], cols)
    ensemble = own_ref.shape[0] - EXTRA
    block = own_ref[:, : own_ref.shape[1] // 2]
    part = grams_of([block], [(0.0, 0.0)], centres_of(INNER + edge_columns))
    for p, ref in enumerate(eight(part_ref)):
        ref[...] = part[p * ensemble : (p + 1) * ensemble]
    for r in range(rows // 8):
        at = slice(r * 8, (r + 1) * 8)
        mean, perturbation = centred(state_ref[at].reshape(8 * cols, ensemble))
        mean_ref[at] = mean.reshape(8, cols, ensemble)
        perturbation_ref[at] = perturbation.reshape(8, cols, ensemble)


def analyse(mean_ref, perturbation_ref, at, across, transform):
    ensemble = transform.shape[0]
    cells = perturbation_ref[at, across, :].reshape(PATCH * PATCH, ensemble)
    change = jnp.dot(cells, transform, preferred_element_type=F32)
    return (mean_ref[at, across, :] + change.reshape(PATCH, PATCH, ensemble)).astype(BF16)


def mid_kernel(odd_ref, column_ref, part_ref, gram, half, z, right, *, tile):
    edge_columns, _ = sides(odd_ref[0], tile[1])
    add_column(list(zip(eight(part_ref), eight(gram))), column_ref, 0.0, centres_of(INNER + edge_columns), float(tile[0]), own=False)
    inner = patches_of(gram, half, z, right)
    for p in inner:
        begin(p)
    advance(inner[:2], inner[2:], (False, False))
    for _ in range(EARLY_STEPS):
        advance(inner[:2], inner[2:])


def edge_kernel(
    odd_ref, far_ref, near_ref, gram_ref, half_ref, z_ref, mean_ref, perturbation_ref, out_ref, gram, half, z, right, done, semaphores
):
    rows, cols, ensemble = mean_ref.shape
    edge_columns, shift = sides(odd_ref[0], cols)
    half[:4] = half_ref[...]
    z[:4] = z_ref[...]
    inner = patches_of(gram_ref.at[:4], half.at[:4], z.at[:4], right.at[:4])
    edge = patches_of(gram, half.at[4:], z.at[4:], right.at[4:])
    for p in inner:
        p.right[...] = side_by_side(p.half[...])
    for at, (ref, col_shift) in enumerate(((near_ref, shift), (far_ref, -shift))):
        pairs = [(gram_ref.at[4 + 2 * r + at], gram.at[2 * r + at]) for r in range(2)]
        add_column(pairs, ref, col_shift, centres_of(edge_columns[at : at + 1]), float(rows))
    traces = [begin(p) for p in edge]

    copies = []

    def put(transforms, columns):
        for p, transform in enumerate(transforms):
            at, across = patch_at(p // 2, columns[p % 2])
            slot = len(copies)
            done[slot] = analyse(mean_ref, perturbation_ref, at, across, transform)
            copies.append(pltpu.make_async_copy(done.at[slot], out_ref.at[at, across, :], semaphores.at[slot]))
            copies[slot].start()

    left = NS_STEPS - 2 - EARLY_STEPS
    for step in range(NS_STEPS - 1):
        with_root = step > 0
        if step < left:
            advance(inner, edge, (True, with_root))
        else:
            advance(edge[:2], edge[2:], (with_root, with_root))
        if step == left:
            put(finish(inner, [system_of(p)[1] for p in inner]), INNER)
    put(finish(edge, traces), edge_columns)
    for copy in copies:
        copy.wait()


def vmem(count):
    return [pl.BlockSpec(memory_space=pltpu.VMEM)] * count


SMEM = pl.BlockSpec(memory_space=pltpu.SMEM)


def pack(members, values, precision, cells, counts, tile_cols):
    capacity, ensemble = members.shape
    given = [pltpu.with_memory_space_constraint(x, pltpu.HBM) for x in (members, values, precision, cells)]
    return pl.pallas_call(
        functools.partial(pack_kernel, tile_cols=tile_cols),
        out_shape=pltpu.VMEM((ensemble + EXTRA, capacity), BF16),
        in_specs=[SMEM] + [pl.BlockSpec(memory_space=pltpu.HBM)] * len(given),
        out_specs=pl.BlockSpec(memory_space=pltpu.VMEM),
        scratch_shapes=[pltpu.VMEM(x.shape, x.dtype) for x in given] + [pltpu.SemaphoreType.DMA((len(given),))],
        compiler_params=pltpu.CompilerParams(vmem_limit_bytes=4 << 20),
    )(counts, *given)


def stack_kernel(own_ref, north_ref, south_ref, late_ref, out_ref, *, tile_rows):
    rows, capacity = own_ref.shape
    kept = capacity // 2
    ensemble = rows - EXTRA
    tiles = (own_ref[...], north_ref[...] + late_ref[...], south_ref[...])
    for at, tile in enumerate(tiles):
        out_ref[:, at * kept : (at + 1) * kept] = tile[:, :kept]
    full = [
        jnp.max(tile[ensemble:, kept:].astype(F32)[WEIGHT : WEIGHT + 1], axis=1, keepdims=True) > 0.0 for tile in tiles[:2]
    ]

    def chosen(own, north, south):
        return jnp.where(full[0], own, jnp.where(full[1], north, south))

    spreads = [tile[:ensemble, kept:].astype(F32) for tile in tiles]
    scalars = [tile[ensemble:, kept:].astype(F32) for tile in tiles]
    index = lax.broadcasted_iota(jnp.int32, (EXTRA, kept), 0)
    shift = chosen(0.0, -float(tile_rows), float(tile_rows))
    out_ref[:ensemble, 3 * kept :] = chosen(*spreads).astype(BF16)
    out_ref[ensemble:, 3 * kept :] = (chosen(*scalars) + jnp.where(index == ROW, shift, 0.0)).astype(BF16)


def stack(own, north, south, late, tile_rows):
    rows, capacity = own.shape
    return pl.pallas_call(
        functools.partial(stack_kernel, tile_rows=tile_rows),
        out_shape=pltpu.VMEM((rows, BLOCKS * (capacity // 2)), BF16),
        in_specs=vmem(4),
        out_specs=pl.BlockSpec(memory_space=pltpu.VMEM),
        compiler_params=pltpu.CompilerParams(vmem_limit_bytes=4 << 20),
    )(own, north, south, late)


def own_part(odd, own, state):
    rows, cols, ensemble = state.shape
    return pl.pallas_call(
        own_kernel,
        out_shape=(
            pltpu.VMEM((8, ensemble, ensemble + EXTRA), F32),
            pltpu.VMEM(state.shape, F32),
            pltpu.VMEM(state.shape, BF16),
        ),
        in_specs=[SMEM] + vmem(2),
        out_specs=tuple(vmem(3)),
        compiler_params=pltpu.CompilerParams(vmem_limit_bytes=12 << 20),
        cost_estimate=pl.CostEstimate(flops=1 << 30, bytes_accessed=1 << 20, transcendentals=0),
    )(odd, own, state)


def middle(odd, column, part, tile):
    ensemble = part.shape[1]
    return pl.pallas_call(
        functools.partial(mid_kernel, tile=tile),
        out_shape=(
            pltpu.VMEM(part.shape, F32),
            pltpu.VMEM((4, ensemble, ensemble), F32),
            pltpu.VMEM((4, ensemble, ensemble), F32),
        ),
        in_specs=[SMEM] + vmem(2),
        out_specs=tuple(vmem(3)),
        scratch_shapes=[pltpu.VMEM((4, ensemble, 2 * ensemble), BF16)],
        compiler_params=pltpu.CompilerParams(vmem_limit_bytes=12 << 20),
        cost_estimate=pl.CostEstimate(flops=1 << 32, bytes_accessed=1 << 20, transcendentals=0),
    )(odd, column, part)


def edges(odd, near, far, gram, half, z, mean, perturbation):
    ensemble = mean.shape[-1]
    return pl.pallas_call(
        edge_kernel,
        out_shape=jax.ShapeDtypeStruct(mean.shape, BF16),
        in_specs=[SMEM] + vmem(7),
        out_specs=pl.BlockSpec(memory_space=pltpu.HBM),
        scratch_shapes=[
            pltpu.VMEM((4, *gram.shape[1:]), F32),
            pltpu.VMEM((8, ensemble, ensemble), F32),
            pltpu.VMEM((8, ensemble, ensemble), F32),
            pltpu.VMEM((8, ensemble, 2 * ensemble), BF16),
            pltpu.VMEM((8, PATCH, PATCH, ensemble), BF16),
            pltpu.SemaphoreType.DMA((8,)),
        ],
        compiler_params=pltpu.CompilerParams(vmem_limit_bytes=12 << 20),
    )(odd, far, near, gram, half, z, mean, perturbation)


def shifts(x):
    count = lax.axis_size("lat")
    upper = count // 2 - 1
    southward = [(i, i + 1) for i in range(count - 1) if i + 1 != upper]
    northward = [(i + 1, i) for i in range(count - 1)]
    return [lax.ppermute(x, "lat", pairs) for pairs in (southward, northward, [(upper - 1, upper)])]


def exchange(x, axis, first):
    count = lax.axis_size(axis)
    pairs = []
    for low in range(first, count, 2):
        high = (low + 1) % count
        pairs += [(low, high), (high, low)]
    return lax.ppermute(x, axis, pairs)


def body(state, obs_members, obs_values, obs_precision, obs_cells, obs_counts):
    _, tile_rows, tile_cols, ensemble = state.shape
    capacity = obs_members.shape[2]
    odd = (lax.axis_index("lon") & 1).astype(jnp.int32).reshape(1)
    own = pack(
        obs_members.reshape(capacity, ensemble),
        obs_values.reshape(1, capacity),
        obs_precision.reshape(1, capacity),
        obs_cells.reshape(1, capacity),
        obs_counts,
        tile_cols,
    )
    column = stack(own, *shifts(own), tile_rows)
    far = exchange(column, "lon", 1)
    near = exchange(column, "lon", 0)
    part, mean, perturbation = own_part(odd, own, state.reshape(tile_rows, tile_cols, ensemble))
    gram, half, z = middle(odd, column, part, (tile_rows, tile_cols))
    out = edges(odd, near, far, gram, half, z, mean, perturbation)
    return out.reshape(state.shape)


def solution(mesh):
    in_specs = (
        P(None, "lat", "lon", None),
        P("lat", "lon", None, None),
        P("lat", "lon", None),
        P("lat", "lon", None),
        P("lat", "lon", None),
        P("lat", "lon"),
    )
    out_specs = P(None, "lat", "lon", None)
    return jax.shard_map(body, mesh=mesh, in_specs=in_specs, out_specs=out_specs, check_vma=False)
```

```python
import functools
from typing import Any, NamedTuple

import jax
import jax.numpy as jnp
from jax import lax
from jax.experimental import pallas as pl
from jax.experimental.pallas import tpu as pltpu
from jax.sharding import PartitionSpec as P

PATCH = 16
NS_STEPS = 12
RAD = 24
EXTRA = 8
WEIGHT, ROW, COL = 2, 5, 6
EARLY_STEPS = 7
INNER = (1, 2)
BLOCKS = 4
F32, BF16 = jnp.float32, jnp.bfloat16


def halves(x):
    high = x.astype(BF16)
    return high, (x - high.astype(F32)).astype(BF16)


def thirds(x):
    high = x.astype(BF16)
    return high, *halves(x - high.astype(F32))


def side_by_side(x):
    return jnp.concatenate(halves(x), axis=1)


def pack_kernel(count_ref, members_in, values_in, precision_in, cells_in, out_ref, *scratch, tile_cols):
    *held, semaphores = scratch
    given = (members_in, values_in, precision_in, cells_in)
    copies = [pltpu.make_async_copy(a, b, semaphores.at[at]) for at, (a, b) in enumerate(zip(given, held))]
    for copy in copies:
        copy.start()
    for copy in copies:
        copy.wait()
    members_ref, values_ref, precision_ref, cells_ref = held
    capacity, ensemble = members_ref.shape
    members = members_ref[...].T.astype(F32)
    mean = jnp.sum(members, axis=0, keepdims=True) * (1.0 / ensemble)
    out_ref[:ensemble, :] = (members - mean).astype(BF16)
    slot = lax.broadcasted_iota(jnp.int32, (1, capacity), 1)
    weight = jnp.where(slot < count_ref[0, 0], precision_ref[...], 0.0)
    cells = cells_ref[...]
    rows = [
        *halves(values_ref[...] - mean),
        *thirds(weight),
        (cells // tile_cols).astype(BF16),
        (cells % tile_cols).astype(BF16),
    ]
    index = lax.broadcasted_iota(jnp.int32, (EXTRA, capacity), 0)
    extra = jnp.zeros((EXTRA, capacity), F32)
    for at, row in enumerate(rows):
        extra = jnp.where(index == at, row.astype(F32), extra)
    out_ref[ensemble:, :] = extra.astype(BF16)


def locals_of(scalars, row_shift, col_shift, centres):
    high, middle, low = (scalars[WEIGHT + at : WEIGHT + at + 1] for at in range(3))
    weight = high + (middle + low)
    rows_twice = 2.0 * (scalars[ROW : ROW + 1] + row_shift) + 1.0
    cols_twice = 2.0 * (scalars[COL : COL + 1] + col_shift) + 1.0
    count = len(centres)
    index = lax.broadcasted_iota(jnp.int32, (8, 1), 0)
    row_centre = jnp.zeros((8, 1), F32)
    col_centre = jnp.zeros((8, 1), F32)
    for at, (row, col) in enumerate(centres):
        row_centre = jnp.where(index == at, row, row_centre)
        col_centre = jnp.where(index == at, col, col_centre)
    row_gap = rows_twice - row_centre
    col_gap = cols_twice - col_centre
    distance = row_gap * row_gap + col_gap * col_gap
    taper = jnp.where(distance < 4.0 * RAD * RAD, jnp.exp(-distance / (2.0 * RAD * RAD)), 0.0)
    local = weight * taper
    return [local[at : at + 1] for at in range(count)]


def grams_of(blocks, shifts, centres):
    ensemble = blocks[0].shape[0] - EXTRA
    weighted = []
    for payload, shift in zip(blocks, shifts):
        spread = payload[:ensemble].astype(F32)
        local = locals_of(payload[ensemble:].astype(F32), *shift, centres)
        weighted.append(jnp.concatenate([(row * spread).astype(BF16) for row in local], axis=0))
    left, right = jnp.concatenate(weighted, axis=1), jnp.concatenate(blocks, axis=1)
    return lax.dot_general(left, right, (((1,), (1,)), ((), ())), preferred_element_type=F32)


def add_column(pairs, column_ref, col_shift, centres, tile_rows, own=True):
    ensemble = column_ref.shape[0] - EXTRA
    kept = column_ref.shape[1] // BLOCKS
    half = len(pairs) // 2
    blocks = [column_ref[:, at * kept : (at + 1) * kept] for at in range(BLOCKS)]
    for at, row_shift in ((0, -tile_rows), (1, tile_rows)):
        here = slice(at * half, (at + 1) * half)
        used = [(blocks[1 + at], row_shift), (blocks[3], 0.0)] + ([(blocks[0], 0.0)] if own else [])
        part = grams_of([block for block, _ in used], [(shift, col_shift) for _, shift in used], centres[here])
        for p, (given, out) in enumerate(pairs[here]):
            out[...] = given[...] + part[p * ensemble : (p + 1) * ensemble]


def double_dot(left, right):
    width = right.shape[1] // 2
    both = jnp.dot(left, jnp.concatenate([right, right], axis=0), preferred_element_type=F32)
    return both[:, :width] + both[:, width:]


class Patch(NamedTuple):
    gram: Any
    half: Any
    z: Any
    right: Any


def patches_of(gram, half, z, right):
    return [Patch(gram.at[p], half.at[p], z.at[p], right.at[p]) for p in range(half.shape[0])]


def diagonal_of(ensemble):
    row = lax.broadcasted_iota(jnp.int32, (ensemble, ensemble), 0)
    return row == lax.broadcasted_iota(jnp.int32, (ensemble, ensemble), 1)


def system_of(patch):
    ensemble = patch.half.shape[0]
    diagonal = diagonal_of(ensemble)
    system = patch.gram[:, :ensemble] + jnp.where(diagonal, ensemble - 1.0, 0.0)
    on = jnp.where(diagonal, system, 0.0)
    return system, jnp.sum(jnp.sum(on, axis=0, keepdims=True), axis=1, keepdims=True)


def begin(patch):
    system, trace = system_of(patch)
    half = system * (-0.5 / trace)
    patch.half[...] = half
    patch.right[...] = side_by_side(half)
    patch.z[...] = jnp.where(diagonal_of(half.shape[0]), 1.5, 0.0) + half
    return trace


def first(patch, with_root):
    right = patch.right[...]
    ensemble = right.shape[0]
    if with_root:
        z = patch.z[...]
        both = double_dot(jnp.concatenate([right, side_by_side(z)], axis=0), right)
        patch.z[...] = 1.5 * z + both[ensemble:]
    else:
        both = double_dot(right, right)
    patch.half[...] = 1.5 * patch.half[...] + both[:ensemble]


def second(patch):
    middle = patch.half[...]
    half = 1.5 * middle + double_dot(side_by_side(middle), patch.right[...])
    patch.half[...] = half
    patch.right[...] = side_by_side(half)


def nothing():
    pass


def advance(some, others, with_root=(True, True), fill=iter(())):
    for p in some:
        first(p, with_root[0])
    next(fill, nothing)()
    for at in range(max(len(some), len(others))):
        if at < len(others):
            first(others[at], with_root[1])
        if at < len(some):
            second(some[at])
        next(fill, nothing)()
    for p in others:
        second(p)


def finish(patches, trace_of, put):
    ensemble = patches[0].half.shape[0]
    column = {}

    def last(at):
        p = patches[at]
        z = p.z[...]
        p.z[...] = 1.5 * z + double_dot(side_by_side(z), p.right[...])

    def times(at):
        across = jnp.sum(jnp.where(diagonal_of(ensemble), column[at], 0.0), axis=0, keepdims=True)
        column[at] = jnp.sum(patches[at].z[...] * across, axis=1, keepdims=True)

    def once(at):
        gram = patches[at].gram
        column[at] = gram[:, ensemble : ensemble + 1] + gram[:, ensemble + 1 : ensemble + 2]
        times(at)

    def use(at):
        trace = trace_of(at)
        scale = jnp.sqrt((ensemble - 1.0) / trace)
        put(at, (patches[at].z[...] * scale + column[at] / trace).astype(BF16))

    return [functools.partial(piece, at) for piece in (last, once, times, use) for at in range(len(patches))]


def centred(cells):
    ensemble = cells.shape[1]
    ones = jnp.full((ensemble, ensemble), 1.0 / ensemble, BF16)
    mean = jnp.dot(cells, ones, preferred_element_type=F32)
    return mean, (cells.astype(F32) - mean).astype(BF16)


def sides(odd, cols):
    last = cols // PATCH - 1
    shift = (1 - 2 * odd).astype(F32) * cols
    return (last * (1 - odd), last * odd), shift


def centre_of(index):
    return jnp.asarray(2 * PATCH * index + PATCH, F32)


def patch_at(r, c):
    return pl.ds(r * PATCH, PATCH), pl.ds(pl.multiple_of(c * PATCH, PATCH), PATCH)


def centres_of(columns):
    return [(centre_of(r), centre_of(c)) for r in range(2) for c in columns]


def eight(ref):
    return [ref.at[4 * edge + 2 * r + at] for r in range(2) for edge in range(2) for at in range(2)]


def own_kernel(odd_ref, own_ref, state_ref, part_ref, mean_ref, perturbation_ref):
    rows, cols, ensemble = state_ref.shape
    edge_columns, _ = sides(odd_ref[0], cols)
    ensemble = own_ref.shape[0] - EXTRA
    block = own_ref[:, : own_ref.shape[1] // 2]
    part = grams_of([block], [(0.0, 0.0)], centres_of(INNER + edge_columns))
    for p, ref in enumerate(eight(part_ref)):
        ref[...] = part[p * ensemble : (p + 1) * ensemble]
    for r in range(rows // 8):
        at = slice(r * 8, (r + 1) * 8)
        mean, perturbation = centred(state_ref[at].reshape(8 * cols, ensemble))
        mean_ref[at] = mean.reshape(8, cols, ensemble)
        perturbation_ref[at] = perturbation.reshape(8, cols, ensemble)


def analyse(mean_ref, perturbation_ref, at, across, transform):
    ensemble = transform.shape[0]
    cells = perturbation_ref[at, across, :].reshape(PATCH * PATCH, ensemble)
    change = jnp.dot(cells, transform, preferred_element_type=F32)
    return (mean_ref[at, across, :] + change.reshape(PATCH, PATCH, ensemble)).astype(BF16)


def mid_kernel(odd_ref, column_ref, part_ref, gram, half, z, right, *, tile):
    edge_columns, _ = sides(odd_ref[0], tile[1])
    add_column(list(zip(eight(part_ref), eight(gram))), column_ref, 0.0, centres_of(INNER + edge_columns), float(tile[0]), own=False)
    inner = patches_of(gram, half, z, right)
    for p in inner:
        begin(p)
    advance(inner[:2], inner[2:], (False, False))
    for _ in range(EARLY_STEPS):
        advance(inner[:2], inner[2:])


def edge_kernel(
    odd_ref, far_ref, near_ref, gram_ref, half_ref, z_ref, mean_ref, perturbation_ref, out_ref, gram, half, z, right, done, semaphores
):
    rows, cols, ensemble = mean_ref.shape
    edge_columns, shift = sides(odd_ref[0], cols)
    half[:4] = half_ref[...]
    z[:4] = z_ref[...]
    inner = patches_of(gram_ref.at[:4], half.at[:4], z.at[:4], right.at[:4])
    edge = patches_of(gram, half.at[4:], z.at[4:], right.at[4:])
    for p in inner:
        p.right[...] = side_by_side(p.half[...])
    columns = []
    for at, (ref, col_shift) in enumerate(((near_ref, shift), (far_ref, -shift))):
        pairs = [(gram_ref.at[4 + 2 * r + at], gram.at[2 * r + at]) for r in range(2)]
        here = centres_of(edge_columns[at : at + 1])
        columns.append(functools.partial(add_column, pairs, ref, col_shift, here, float(rows)))
    advance(inner[:2], inner[2:], fill=iter(columns))
    traces = [begin(p) for p in edge]

    copies = []

    def put(place, at, transform):
        band, across = patch_at(at // 2, place[at % 2])
        slot = len(copies)
        done[slot] = analyse(mean_ref, perturbation_ref, band, across, transform)
        copies.append(pltpu.make_async_copy(done.at[slot], out_ref.at[band, across, :], semaphores.at[slot]))
        copies[slot].start()

    left = NS_STEPS - 3 - EARLY_STEPS
    pieces = iter(finish(inner, lambda at: system_of(inner[at])[1], functools.partial(put, INNER)))
    for step in range(NS_STEPS - 1):
        with_root = step > 0
        if step < left:
            advance(inner, edge, (True, with_root))
        else:
            advance(edge[:2], edge[2:], (with_root, with_root), pieces)
    for piece in pieces:
        piece()
    for piece in finish(edge, lambda at: traces[at], functools.partial(put, edge_columns)):
        piece()
    for copy in copies:
        copy.wait()


def vmem(count):
    return [pl.BlockSpec(memory_space=pltpu.VMEM)] * count


SMEM = pl.BlockSpec(memory_space=pltpu.SMEM)


def pack(members, values, precision, cells, counts, tile_cols):
    capacity, ensemble = members.shape
    given = [pltpu.with_memory_space_constraint(x, pltpu.HBM) for x in (members, values, precision, cells)]
    return pl.pallas_call(
        functools.partial(pack_kernel, tile_cols=tile_cols),
        out_shape=pltpu.VMEM((ensemble + EXTRA, capacity), BF16),
        in_specs=[SMEM] + [pl.BlockSpec(memory_space=pltpu.HBM)] * len(given),
        out_specs=pl.BlockSpec(memory_space=pltpu.VMEM),
        scratch_shapes=[pltpu.VMEM(x.shape, x.dtype) for x in given] + [pltpu.SemaphoreType.DMA((len(given),))],
        compiler_params=pltpu.CompilerParams(vmem_limit_bytes=4 << 20),
    )(counts, *given)


def stack_kernel(own_ref, north_ref, south_ref, late_ref, out_ref, *, tile_rows):
    rows, capacity = own_ref.shape
    kept = capacity // 2
    ensemble = rows - EXTRA
    tiles = (own_ref[...], north_ref[...] + late_ref[...], south_ref[...])
    for at, tile in enumerate(tiles):
        out_ref[:, at * kept : (at + 1) * kept] = tile[:, :kept]
    full = [
        jnp.max(tile[ensemble:, kept:].astype(F32)[WEIGHT : WEIGHT + 1], axis=1, keepdims=True) > 0.0 for tile in tiles[:2]
    ]

    def chosen(own, north, south):
        return jnp.where(full[0], own, jnp.where(full[1], north, south))

    spreads = [tile[:ensemble, kept:].astype(F32) for tile in tiles]
    scalars = [tile[ensemble:, kept:].astype(F32) for tile in tiles]
    index = lax.broadcasted_iota(jnp.int32, (EXTRA, kept), 0)
    shift = chosen(0.0, -float(tile_rows), float(tile_rows))
    out_ref[:ensemble, 3 * kept :] = chosen(*spreads).astype(BF16)
    out_ref[ensemble:, 3 * kept :] = (chosen(*scalars) + jnp.where(index == ROW, shift, 0.0)).astype(BF16)


def stack(own, north, south, late, tile_rows):
    rows, capacity = own.shape
    return pl.pallas_call(
        functools.partial(stack_kernel, tile_rows=tile_rows),
        out_shape=pltpu.VMEM((rows, BLOCKS * (capacity // 2)), BF16),
        in_specs=vmem(4),
        out_specs=pl.BlockSpec(memory_space=pltpu.VMEM),
        compiler_params=pltpu.CompilerParams(vmem_limit_bytes=4 << 20),
    )(own, north, south, late)


def own_part(odd, own, state):
    rows, cols, ensemble = state.shape
    return pl.pallas_call(
        own_kernel,
        out_shape=(
            pltpu.VMEM((8, ensemble, ensemble + EXTRA), F32),
            pltpu.VMEM(state.shape, F32),
            pltpu.VMEM(state.shape, BF16),
        ),
        in_specs=[SMEM] + vmem(2),
        out_specs=tuple(vmem(3)),
        compiler_params=pltpu.CompilerParams(vmem_limit_bytes=12 << 20),
        cost_estimate=pl.CostEstimate(flops=1 << 30, bytes_accessed=1 << 20, transcendentals=0),
    )(odd, own, state)


def middle(odd, column, part, tile):
    ensemble = part.shape[1]
    return pl.pallas_call(
        functools.partial(mid_kernel, tile=tile),
        out_shape=(
            pltpu.VMEM(part.shape, F32),
            pltpu.VMEM((4, ensemble, ensemble), F32),
            pltpu.VMEM((4, ensemble, ensemble), F32),
        ),
        in_specs=[SMEM] + vmem(2),
        out_specs=tuple(vmem(3)),
        scratch_shapes=[pltpu.VMEM((4, ensemble, 2 * ensemble), BF16)],
        compiler_params=pltpu.CompilerParams(vmem_limit_bytes=12 << 20),
        cost_estimate=pl.CostEstimate(flops=1 << 32, bytes_accessed=1 << 20, transcendentals=0),
    )(odd, column, part)


def edges(odd, near, far, gram, half, z, mean, perturbation):
    ensemble = mean.shape[-1]
    return pl.pallas_call(
        edge_kernel,
        out_shape=jax.ShapeDtypeStruct(mean.shape, BF16),
        in_specs=[SMEM] + vmem(7),
        out_specs=pl.BlockSpec(memory_space=pltpu.HBM),
        scratch_shapes=[
            pltpu.VMEM((4, *gram.shape[1:]), F32),
            pltpu.VMEM((8, ensemble, ensemble), F32),
            pltpu.VMEM((8, ensemble, ensemble), F32),
            pltpu.VMEM((8, ensemble, 2 * ensemble), BF16),
            pltpu.VMEM((8, PATCH, PATCH, ensemble), BF16),
            pltpu.SemaphoreType.DMA((8,)),
        ],
        compiler_params=pltpu.CompilerParams(vmem_limit_bytes=12 << 20),
    )(odd, far, near, gram, half, z, mean, perturbation)


def shifts(x):
    count = lax.axis_size("lat")
    upper = count // 2 - 1
    southward = [(i, i + 1) for i in range(count - 1) if i + 1 != upper]
    northward = [(i + 1, i) for i in range(count - 1)]
    return [lax.ppermute(x, "lat", pairs) for pairs in (southward, northward, [(upper - 1, upper)])]


def exchange(x, axis, first):
    count = lax.axis_size(axis)
    pairs = []
    for low in range(first, count, 2):
        high = (low + 1) % count
        pairs += [(low, high), (high, low)]
    return lax.ppermute(x, axis, pairs)


def body(state, obs_members, obs_values, obs_precision, obs_cells, obs_counts):
    _, tile_rows, tile_cols, ensemble = state.shape
    capacity = obs_members.shape[2]
    odd = (lax.axis_index("lon") & 1).astype(jnp.int32).reshape(1)
    own = pack(
        obs_members.reshape(capacity, ensemble),
        obs_values.reshape(1, capacity),
        obs_precision.reshape(1, capacity),
        obs_cells.reshape(1, capacity),
        obs_counts,
        tile_cols,
    )
    column = stack(own, *shifts(own), tile_rows)
    far = exchange(column, "lon", 1)
    near = exchange(column, "lon", 0)
    part, mean, perturbation = own_part(odd, own, state.reshape(tile_rows, tile_cols, ensemble))
    gram, half, z = middle(odd, column, part, (tile_rows, tile_cols))
    out = edges(odd, near, far, gram, half, z, mean, perturbation)
    return out.reshape(state.shape)


def solution(mesh):
    in_specs = (
        P(None, "lat", "lon", None),
        P("lat", "lon", None, None),
        P("lat", "lon", None),
        P("lat", "lon", None),
        P("lat", "lon", None),
        P("lat", "lon"),
    )
    out_specs = P(None, "lat", "lon", None)
    return jax.shard_map(body, mesh=mesh, in_specs=in_specs, out_specs=out_specs, check_vma=False)
```

```python
import functools
from typing import Any, NamedTuple

import jax
import jax.numpy as jnp
from jax import lax
from jax.experimental import pallas as pl
from jax.experimental.pallas import tpu as pltpu
from jax.sharding import PartitionSpec as P

PATCH = 16
NS_STEPS = 12
RAD = 24
EXTRA = 8
WEIGHT, ROW, COL = 2, 5, 6
EARLY_STEPS = 6
INNER = (1, 2)
BLOCKS = 4
F32, BF16 = jnp.float32, jnp.bfloat16


def halves(x):
    high = x.astype(BF16)
    return high, (x - high.astype(F32)).astype(BF16)


def thirds(x):
    high = x.astype(BF16)
    return high, *halves(x - high.astype(F32))


def side_by_side(x):
    return jnp.concatenate(halves(x), axis=1)


def pack_kernel(count_ref, members_in, values_in, precision_in, cells_in, out_ref, *scratch, tile_cols):
    *held, semaphores = scratch
    given = (members_in, values_in, precision_in, cells_in)
    copies = [pltpu.make_async_copy(a, b, semaphores.at[at]) for at, (a, b) in enumerate(zip(given, held))]
    for copy in copies:
        copy.start()
    for copy in copies:
        copy.wait()
    members_ref, values_ref, precision_ref, cells_ref = held
    capacity, ensemble = members_ref.shape
    members = members_ref[...].T.astype(F32)
    mean = jnp.sum(members, axis=0, keepdims=True) * (1.0 / ensemble)
    out_ref[:ensemble, :] = (members - mean).astype(BF16)
    slot = lax.broadcasted_iota(jnp.int32, (1, capacity), 1)
    weight = jnp.where(slot < count_ref[0, 0], precision_ref[...], 0.0)
    cells = cells_ref[...]
    rows = [
        *halves(values_ref[...] - mean),
        *thirds(weight),
        (cells // tile_cols).astype(BF16),
        (cells % tile_cols).astype(BF16),
    ]
    index = lax.broadcasted_iota(jnp.int32, (EXTRA, capacity), 0)
    extra = jnp.zeros((EXTRA, capacity), F32)
    for at, row in enumerate(rows):
        extra = jnp.where(index == at, row.astype(F32), extra)
    out_ref[ensemble:, :] = extra.astype(BF16)


def locals_of(scalars, row_shift, col_shift, centres):
    high, middle, low = (scalars[WEIGHT + at : WEIGHT + at + 1] for at in range(3))
    weight = high + (middle + low)
    rows_twice = 2.0 * (scalars[ROW : ROW + 1] + row_shift) + 1.0
    cols_twice = 2.0 * (scalars[COL : COL + 1] + col_shift) + 1.0
    count = len(centres)
    index = lax.broadcasted_iota(jnp.int32, (8, 1), 0)
    row_centre = jnp.zeros((8, 1), F32)
    col_centre = jnp.zeros((8, 1), F32)
    for at, (row, col) in enumerate(centres):
        row_centre = jnp.where(index == at, row, row_centre)
        col_centre = jnp.where(index == at, col, col_centre)
    row_gap = rows_twice - row_centre
    col_gap = cols_twice - col_centre
    distance = row_gap * row_gap + col_gap * col_gap
    taper = jnp.where(distance < 4.0 * RAD * RAD, jnp.exp(-distance / (2.0 * RAD * RAD)), 0.0)
    local = weight * taper
    return [local[at : at + 1] for at in range(count)]


def grams_of(blocks, shifts, centres):
    ensemble = blocks[0].shape[0] - EXTRA
    weighted = []
    for payload, shift in zip(blocks, shifts):
        spread = payload[:ensemble].astype(F32)
        local = locals_of(payload[ensemble:].astype(F32), *shift, centres)
        weighted.append(jnp.concatenate([(row * spread).astype(BF16) for row in local], axis=0))
    left, right = jnp.concatenate(weighted, axis=1), jnp.concatenate(blocks, axis=1)
    return lax.dot_general(left, right, (((1,), (1,)), ((), ())), preferred_element_type=F32)


def add_column(pairs, column_ref, col_shift, centres, tile_rows, own=True):
    ensemble = column_ref.shape[0] - EXTRA
    kept = column_ref.shape[1] // BLOCKS
    half = len(pairs) // 2
    blocks = [column_ref[:, at * kept : (at + 1) * kept] for at in range(BLOCKS)]
    for at, row_shift in ((0, -tile_rows), (1, tile_rows)):
        here = slice(at * half, (at + 1) * half)
        used = [(blocks[1 + at], row_shift), (blocks[3], 0.0)] + ([(blocks[0], 0.0)] if own else [])
        part = grams_of([block for block, _ in used], [(shift, col_shift) for _, shift in used], centres[here])
        for p, (given, out) in enumerate(pairs[here]):
            out[...] = given[...] + part[p * ensemble : (p + 1) * ensemble]


def double_dot(left, right):
    width = right.shape[1] // 2
    both = jnp.dot(left, jnp.concatenate([right, right], axis=0), preferred_element_type=F32)
    return both[:, :width] + both[:, width:]


class Patch(NamedTuple):
    gram: Any
    half: Any
    z: Any
    right: Any


def patches_of(gram, half, z, right):
    return [Patch(gram.at[p], half.at[p], z.at[p], right.at[p]) for p in range(half.shape[0])]


def diagonal_of(ensemble):
    row = lax.broadcasted_iota(jnp.int32, (ensemble, ensemble), 0)
    return row == lax.broadcasted_iota(jnp.int32, (ensemble, ensemble), 1)


def system_of(patch):
    ensemble = patch.half.shape[0]
    diagonal = diagonal_of(ensemble)
    system = patch.gram[:, :ensemble] + jnp.where(diagonal, ensemble - 1.0, 0.0)
    on = jnp.where(diagonal, system, 0.0)
    return system, jnp.sum(jnp.sum(on, axis=0, keepdims=True), axis=1, keepdims=True)


def begin(patch):
    system, trace = system_of(patch)
    half = system * (-0.5 / trace)
    patch.half[...] = half
    patch.right[...] = side_by_side(half)
    patch.z[...] = jnp.where(diagonal_of(half.shape[0]), 1.5, 0.0) + half
    return trace


def first(patch, with_root):
    right = patch.right[...]
    ensemble = right.shape[0]
    if with_root:
        z = patch.z[...]
        both = double_dot(jnp.concatenate([right, side_by_side(z)], axis=0), right)
        patch.z[...] = 1.5 * z + both[ensemble:]
    else:
        both = double_dot(right, right)
    patch.half[...] = 1.5 * patch.half[...] + both[:ensemble]


def second(patch):
    middle = patch.half[...]
    half = 1.5 * middle + double_dot(side_by_side(middle), patch.right[...])
    patch.half[...] = half
    patch.right[...] = side_by_side(half)


def nothing():
    pass


def advance(some, others, with_root=(True, True), fill=iter(())):
    for p in some:
        first(p, with_root[0])
    next(fill, nothing)()
    for at in range(max(len(some), len(others))):
        if at < len(others):
            first(others[at], with_root[1])
        if at < len(some):
            second(some[at])
        next(fill, nothing)()
    for p in others:
        second(p)


def finish(patches, trace_of, put):
    ensemble = patches[0].half.shape[0]
    column = {}

    def last(at):
        p = patches[at]
        z = p.z[...]
        p.z[...] = 1.5 * z + double_dot(side_by_side(z), p.right[...])

    def times(at):
        across = jnp.sum(jnp.where(diagonal_of(ensemble), column[at], 0.0), axis=0, keepdims=True)
        column[at] = jnp.sum(patches[at].z[...] * across, axis=1, keepdims=True)

    def once(at):
        gram = patches[at].gram
        column[at] = gram[:, ensemble : ensemble + 1] + gram[:, ensemble + 1 : ensemble + 2]
        times(at)

    def use(at):
        trace = trace_of(at)
        scale = jnp.sqrt((ensemble - 1.0) / trace)
        put(at, (patches[at].z[...] * scale + column[at] / trace).astype(BF16))

    return [functools.partial(piece, at) for piece in (last, once, times, use) for at in range(len(patches))]


def centred(cells):
    ensemble = cells.shape[1]
    ones = jnp.full((ensemble, ensemble), 1.0 / ensemble, BF16)
    mean = jnp.dot(cells, ones, preferred_element_type=F32)
    return mean, (cells.astype(F32) - mean).astype(BF16)


def sides(odd, cols):
    last = cols // PATCH - 1
    shift = (1 - 2 * odd).astype(F32) * cols
    return (last * (1 - odd), last * odd), shift


def centre_of(index):
    return jnp.asarray(2 * PATCH * index + PATCH, F32)


def patch_at(r, c):
    return pl.ds(r * PATCH, PATCH), pl.ds(pl.multiple_of(c * PATCH, PATCH), PATCH)


def centres_of(columns):
    return [(centre_of(r), centre_of(c)) for r in range(2) for c in columns]


def eight(ref):
    return [ref.at[4 * edge + 2 * r + at] for r in range(2) for edge in range(2) for at in range(2)]


def own_kernel(odd_ref, own_ref, state_ref, part_ref, mean_ref, perturbation_ref):
    rows, cols, ensemble = state_ref.shape
    edge_columns, _ = sides(odd_ref[0], cols)
    ensemble = own_ref.shape[0] - EXTRA
    block = own_ref[:, : own_ref.shape[1] // 2]
    part = grams_of([block], [(0.0, 0.0)], centres_of(INNER + edge_columns))
    for p, ref in enumerate(eight(part_ref)):
        ref[...] = part[p * ensemble : (p + 1) * ensemble]
    for r in range(rows // 8):
        at = slice(r * 8, (r + 1) * 8)
        mean, perturbation = centred(state_ref[at].reshape(8 * cols, ensemble))
        mean_ref[at] = mean.reshape(8, cols, ensemble)
        perturbation_ref[at] = perturbation.reshape(8, cols, ensemble)


def analyse(mean_ref, perturbation_ref, at, across, transform):
    ensemble = transform.shape[0]
    cells = perturbation_ref[at, across, :].reshape(PATCH * PATCH, ensemble)
    change = jnp.dot(cells, transform, preferred_element_type=F32)
    return (mean_ref[at, across, :] + change.reshape(PATCH, PATCH, ensemble)).astype(BF16)


def mid_kernel(odd_ref, column_ref, part_ref, gram, half, z, right, *, tile):
    edge_columns, _ = sides(odd_ref[0], tile[1])
    add_column(list(zip(eight(part_ref), eight(gram))), column_ref, 0.0, centres_of(INNER + edge_columns), float(tile[0]), own=False)
    inner = patches_of(gram, half, z, right)
    for p in inner:
        begin(p)
    advance(inner[:2], inner[2:], (False, False))
    for _ in range(EARLY_STEPS):
        advance(inner[:2], inner[2:])


def edge_kernel(
    odd_ref, far_ref, near_ref, gram_ref, half_ref, z_ref, mean_ref, perturbation_ref, out_ref, gram, half, z, right, done, semaphores
):
    rows, cols, ensemble = mean_ref.shape
    edge_columns, shift = sides(odd_ref[0], cols)
    half[:4] = half_ref[...]
    z[:4] = z_ref[...]
    inner = patches_of(gram_ref.at[:4], half.at[:4], z.at[:4], right.at[:4])
    edge = patches_of(gram, half.at[4:], z.at[4:], right.at[4:])
    for p in inner:
        p.right[...] = side_by_side(p.half[...])
    columns = []
    for at, (ref, col_shift) in enumerate(((near_ref, shift), (far_ref, -shift))):
        pairs = [(gram_ref.at[4 + 2 * r + at], gram.at[2 * r + at]) for r in range(2)]
        here = centres_of(edge_columns[at : at + 1])
        columns.append(functools.partial(add_column, pairs, ref, col_shift, here, float(rows)))
    advance(inner[:2], inner[2:], fill=iter(columns))
    traces = [begin(p) for p in edge]

    copies = []

    def put(place, at, transform):
        band, across = patch_at(at // 2, place[at % 2])
        slot = len(copies)
        done[slot] = analyse(mean_ref, perturbation_ref, band, across, transform)
        copies.append(pltpu.make_async_copy(done.at[slot], out_ref.at[band, across, :], semaphores.at[slot]))
        copies[slot].start()

    left = NS_STEPS - 3 - EARLY_STEPS
    pieces = iter(finish(inner, lambda at: system_of(inner[at])[1], functools.partial(put, INNER)))
    for step in range(NS_STEPS - 1):
        with_root = step > 0
        if step < left:
            advance(inner, edge, (True, with_root))
        else:
            advance(edge[:2], edge[2:], (with_root, with_root), pieces)
    for piece in pieces:
        piece()
    for piece in finish(edge, lambda at: traces[at], functools.partial(put, edge_columns)):
        piece()
    for copy in copies:
        copy.wait()


def vmem(count):
    return [pl.BlockSpec(memory_space=pltpu.VMEM)] * count


SMEM = pl.BlockSpec(memory_space=pltpu.SMEM)


def pack(members, values, precision, cells, counts, tile_cols):
    capacity, ensemble = members.shape
    given = [pltpu.with_memory_space_constraint(x, pltpu.HBM) for x in (members, values, precision, cells)]
    return pl.pallas_call(
        functools.partial(pack_kernel, tile_cols=tile_cols),
        out_shape=pltpu.VMEM((ensemble + EXTRA, capacity), BF16),
        in_specs=[SMEM] + [pl.BlockSpec(memory_space=pltpu.HBM)] * len(given),
        out_specs=pl.BlockSpec(memory_space=pltpu.VMEM),
        scratch_shapes=[pltpu.VMEM(x.shape, x.dtype) for x in given] + [pltpu.SemaphoreType.DMA((len(given),))],
        compiler_params=pltpu.CompilerParams(vmem_limit_bytes=4 << 20),
    )(counts, *given)


def stack_kernel(own_ref, north_ref, south_ref, late_ref, out_ref, *, tile_rows):
    rows, capacity = own_ref.shape
    kept = capacity // 2
    ensemble = rows - EXTRA
    tiles = (own_ref[...], north_ref[...] + late_ref[...], south_ref[...])
    for at, tile in enumerate(tiles):
        out_ref[:, at * kept : (at + 1) * kept] = tile[:, :kept]
    full = [
        jnp.max(tile[ensemble:, kept:].astype(F32)[WEIGHT : WEIGHT + 1], axis=1, keepdims=True) > 0.0 for tile in tiles[:2]
    ]

    def chosen(own, north, south):
        return jnp.where(full[0], own, jnp.where(full[1], north, south))

    spreads = [tile[:ensemble, kept:].astype(F32) for tile in tiles]
    scalars = [tile[ensemble:, kept:].astype(F32) for tile in tiles]
    index = lax.broadcasted_iota(jnp.int32, (EXTRA, kept), 0)
    shift = chosen(0.0, -float(tile_rows), float(tile_rows))
    out_ref[:ensemble, 3 * kept :] = chosen(*spreads).astype(BF16)
    out_ref[ensemble:, 3 * kept :] = (chosen(*scalars) + jnp.where(index == ROW, shift, 0.0)).astype(BF16)


def stack(own, north, south, late, tile_rows):
    rows, capacity = own.shape
    return pl.pallas_call(
        functools.partial(stack_kernel, tile_rows=tile_rows),
        out_shape=pltpu.VMEM((rows, BLOCKS * (capacity // 2)), BF16),
        in_specs=vmem(4),
        out_specs=pl.BlockSpec(memory_space=pltpu.VMEM),
        compiler_params=pltpu.CompilerParams(vmem_limit_bytes=4 << 20),
    )(own, north, south, late)


def own_part(odd, own, state):
    rows, cols, ensemble = state.shape
    return pl.pallas_call(
        own_kernel,
        out_shape=(
            pltpu.VMEM((8, ensemble, ensemble + EXTRA), F32),
            pltpu.VMEM(state.shape, F32),
            pltpu.VMEM(state.shape, BF16),
        ),
        in_specs=[SMEM] + vmem(2),
        out_specs=tuple(vmem(3)),
        compiler_params=pltpu.CompilerParams(vmem_limit_bytes=12 << 20),
        cost_estimate=pl.CostEstimate(flops=1 << 30, bytes_accessed=1 << 20, transcendentals=0),
    )(odd, own, state)


def middle(odd, column, part, tile):
    ensemble = part.shape[1]
    return pl.pallas_call(
        functools.partial(mid_kernel, tile=tile),
        out_shape=(
            pltpu.VMEM(part.shape, F32),
            pltpu.VMEM((4, ensemble, ensemble), F32),
            pltpu.VMEM((4, ensemble, ensemble), F32),
        ),
        in_specs=[SMEM] + vmem(2),
        out_specs=tuple(vmem(3)),
        scratch_shapes=[pltpu.VMEM((4, ensemble, 2 * ensemble), BF16)],
        compiler_params=pltpu.CompilerParams(vmem_limit_bytes=12 << 20),
        cost_estimate=pl.CostEstimate(flops=1 << 32, bytes_accessed=1 << 20, transcendentals=0),
    )(odd, column, part)


def edges(odd, near, far, gram, half, z, mean, perturbation):
    ensemble = mean.shape[-1]
    return pl.pallas_call(
        edge_kernel,
        out_shape=jax.ShapeDtypeStruct(mean.shape, BF16),
        in_specs=[SMEM] + vmem(7),
        out_specs=pl.BlockSpec(memory_space=pltpu.HBM),
        scratch_shapes=[
            pltpu.VMEM((4, *gram.shape[1:]), F32),
            pltpu.VMEM((8, ensemble, ensemble), F32),
            pltpu.VMEM((8, ensemble, ensemble), F32),
            pltpu.VMEM((8, ensemble, 2 * ensemble), BF16),
            pltpu.VMEM((8, PATCH, PATCH, ensemble), BF16),
            pltpu.SemaphoreType.DMA((8,)),
        ],
        compiler_params=pltpu.CompilerParams(vmem_limit_bytes=12 << 20),
    )(odd, far, near, gram, half, z, mean, perturbation)


def shifts(x):
    count = lax.axis_size("lat")
    upper = count // 2 - 1
    southward = [(i, i + 1) for i in range(count - 1) if i + 1 != upper]
    northward = [(i + 1, i) for i in range(count - 1)]
    return [lax.ppermute(x, "lat", pairs) for pairs in (southward, northward, [(upper - 1, upper)])]


def exchange(x, axis, first):
    count = lax.axis_size(axis)
    pairs = []
    for low in range(first, count, 2):
        high = (low + 1) % count
        pairs += [(low, high), (high, low)]
    return lax.ppermute(x, axis, pairs)


def body(state, obs_members, obs_values, obs_precision, obs_cells, obs_counts):
    _, tile_rows, tile_cols, ensemble = state.shape
    capacity = obs_members.shape[2]
    odd = (lax.axis_index("lon") & 1).astype(jnp.int32).reshape(1)
    own = pack(
        obs_members.reshape(capacity, ensemble),
        obs_values.reshape(1, capacity),
        obs_precision.reshape(1, capacity),
        obs_cells.reshape(1, capacity),
        obs_counts,
        tile_cols,
    )
    column = stack(own, *shifts(own), tile_rows)
    far = exchange(column, "lon", 1)
    near = exchange(column, "lon", 0)
    part, mean, perturbation = own_part(odd, own, state.reshape(tile_rows, tile_cols, ensemble))
    gram, half, z = middle(odd, column, part, (tile_rows, tile_cols))
    out = edges(odd, near, far, gram, half, z, mean, perturbation)
    return out.reshape(state.shape)


def solution(mesh):
    in_specs = (
        P(None, "lat", "lon", None),
        P("lat", "lon", None, None),
        P("lat", "lon", None),
        P("lat", "lon", None),
        P("lat", "lon", None),
        P("lat", "lon"),
    )
    out_specs = P(None, "lat", "lon", None)
    return jax.shard_map(body, mesh=mesh, in_specs=in_specs, out_specs=out_specs, check_vma=False)
```

```python
import functools
from typing import Any, NamedTuple

import jax
import jax.numpy as jnp
from jax import lax
from jax.experimental import pallas as pl
from jax.experimental.pallas import tpu as pltpu
from jax.sharding import PartitionSpec as P

PATCH = 16
NS_STEPS = 12
RAD = 24
EXTRA = 8
WEIGHT, ROW, COL = 2, 5, 6
EARLY_STEPS = 4
INNER = (1, 2)
BLOCKS = 4
F32, BF16 = jnp.float32, jnp.bfloat16


def halves(x):
    high = x.astype(BF16)
    return high, (x - high.astype(F32)).astype(BF16)


def thirds(x):
    high = x.astype(BF16)
    return high, *halves(x - high.astype(F32))


def side_by_side(x):
    return jnp.concatenate(halves(x), axis=1)


def pack_kernel(count_ref, members_in, values_in, precision_in, cells_in, out_ref, *scratch, tile_cols):
    *held, semaphores = scratch
    given = (members_in, values_in, precision_in, cells_in)
    copies = [pltpu.make_async_copy(a, b, semaphores.at[at]) for at, (a, b) in enumerate(zip(given, held))]
    for copy in copies:
        copy.start()
    for copy in copies:
        copy.wait()
    members_ref, values_ref, precision_ref, cells_ref = held
    capacity, ensemble = members_ref.shape
    members = members_ref[...].T.astype(F32)
    mean = jnp.sum(members, axis=0, keepdims=True) * (1.0 / ensemble)
    out_ref[:ensemble, :] = (members - mean).astype(BF16)
    slot = lax.broadcasted_iota(jnp.int32, (1, capacity), 1)
    weight = jnp.where(slot < count_ref[0, 0], precision_ref[...], 0.0)
    cells = cells_ref[...]
    rows = [
        *halves(values_ref[...] - mean),
        *thirds(weight),
        (cells // tile_cols).astype(BF16),
        (cells % tile_cols).astype(BF16),
    ]
    index = lax.broadcasted_iota(jnp.int32, (EXTRA, capacity), 0)
    extra = jnp.zeros((EXTRA, capacity), F32)
    for at, row in enumerate(rows):
        extra = jnp.where(index == at, row.astype(F32), extra)
    out_ref[ensemble:, :] = extra.astype(BF16)


def locals_of(scalars, row_shift, col_shift, centres):
    high, middle, low = (scalars[WEIGHT + at : WEIGHT + at + 1] for at in range(3))
    weight = high + (middle + low)
    rows_twice = 2.0 * (scalars[ROW : ROW + 1] + row_shift) + 1.0
    cols_twice = 2.0 * (scalars[COL : COL + 1] + col_shift) + 1.0
    count = len(centres)
    index = lax.broadcasted_iota(jnp.int32, (8, 1), 0)
    row_centre = jnp.zeros((8, 1), F32)
    col_centre = jnp.zeros((8, 1), F32)
    for at, (row, col) in enumerate(centres):
        row_centre = jnp.where(index == at, row, row_centre)
        col_centre = jnp.where(index == at, col, col_centre)
    row_gap = rows_twice - row_centre
    col_gap = cols_twice - col_centre
    distance = row_gap * row_gap + col_gap * col_gap
    taper = jnp.where(distance < 4.0 * RAD * RAD, jnp.exp(-distance / (2.0 * RAD * RAD)), 0.0)
    local = weight * taper
    return [local[at : at + 1] for at in range(count)]


def grams_of(blocks, shifts, centres):
    ensemble = blocks[0].shape[0] - EXTRA
    weighted = []
    for payload, shift in zip(blocks, shifts):
        spread = payload[:ensemble].astype(F32)
        local = locals_of(payload[ensemble:].astype(F32), *shift, centres)
        weighted.append(jnp.concatenate([(row * spread).astype(BF16) for row in local], axis=0))
    left, right = jnp.concatenate(weighted, axis=1), jnp.concatenate(blocks, axis=1)
    return lax.dot_general(left, right, (((1,), (1,)), ((), ())), preferred_element_type=F32)


def add_column(pairs, column_ref, col_shift, centres, tile_rows, own=True):
    ensemble = column_ref.shape[0] - EXTRA
    kept = column_ref.shape[1] // BLOCKS
    half = len(pairs) // 2
    blocks = [column_ref[:, at * kept : (at + 1) * kept] for at in range(BLOCKS)]
    for at, row_shift in ((0, -tile_rows), (1, tile_rows)):
        here = slice(at * half, (at + 1) * half)
        used = [(blocks[1 + at], row_shift), (blocks[3], 0.0)] + ([(blocks[0], 0.0)] if own else [])
        part = grams_of([block for block, _ in used], [(shift, col_shift) for _, shift in used], centres[here])
        for p, (given, out) in enumerate(pairs[here]):
            out[...] = given[...] + part[p * ensemble : (p + 1) * ensemble]


def double_dot(left, right):
    width = right.shape[1] // 2
    both = jnp.dot(left, jnp.concatenate([right, right], axis=0), preferred_element_type=F32)
    return both[:, :width] + both[:, width:]


class Patch(NamedTuple):
    gram: Any
    half: Any
    z: Any
    right: Any


def patches_of(gram, half, z, right):
    return [Patch(gram.at[p], half.at[p], z.at[p], right.at[p]) for p in range(half.shape[0])]


def diagonal_of(ensemble):
    row = lax.broadcasted_iota(jnp.int32, (ensemble, ensemble), 0)
    return row == lax.broadcasted_iota(jnp.int32, (ensemble, ensemble), 1)


def system_of(patch):
    ensemble = patch.half.shape[0]
    diagonal = diagonal_of(ensemble)
    system = patch.gram[:, :ensemble] + jnp.where(diagonal, ensemble - 1.0, 0.0)
    on = jnp.where(diagonal, system, 0.0)
    return system, jnp.sum(jnp.sum(on, axis=0, keepdims=True), axis=1, keepdims=True)


def begin(patch):
    system, trace = system_of(patch)
    half = system * (-0.5 / trace)
    patch.half[...] = half
    patch.right[...] = side_by_side(half)
    patch.z[...] = jnp.where(diagonal_of(half.shape[0]), 1.5, 0.0) + half
    return trace


def first(patch, with_root):
    right = patch.right[...]
    ensemble = right.shape[0]
    if with_root:
        z = patch.z[...]
        both = double_dot(jnp.concatenate([right, side_by_side(z)], axis=0), right)
        patch.z[...] = 1.5 * z + both[ensemble:]
    else:
        both = double_dot(right, right)
    patch.half[...] = 1.5 * patch.half[...] + both[:ensemble]


def second(patch):
    middle = patch.half[...]
    half = 1.5 * middle + double_dot(side_by_side(middle), patch.right[...])
    patch.half[...] = half
    patch.right[...] = side_by_side(half)


def nothing():
    pass


def advance(some, others, with_root=(True, True), fill=iter(())):
    for p in some:
        first(p, with_root[0])
    next(fill, nothing)()
    for at in range(max(len(some), len(others))):
        if at < len(others):
            first(others[at], with_root[1])
        if at < len(some):
            second(some[at])
        next(fill, nothing)()
    for p in others:
        second(p)


def finish(patches, trace_of, put):
    ensemble = patches[0].half.shape[0]
    column = {}

    def last(at):
        p = patches[at]
        z = p.z[...]
        p.z[...] = 1.5 * z + double_dot(side_by_side(z), p.right[...])

    def times(at):
        across = jnp.sum(jnp.where(diagonal_of(ensemble), column[at], 0.0), axis=0, keepdims=True)
        column[at] = jnp.sum(patches[at].z[...] * across, axis=1, keepdims=True)

    def once(at):
        gram = patches[at].gram
        column[at] = gram[:, ensemble : ensemble + 1] + gram[:, ensemble + 1 : ensemble + 2]
        times(at)

    def use(at):
        trace = trace_of(at)
        scale = jnp.sqrt((ensemble - 1.0) / trace)
        put(at, (patches[at].z[...] * scale + column[at] / trace).astype(BF16))

    return [functools.partial(piece, at) for piece in (last, once, times, use) for at in range(len(patches))]


def centred(cells):
    ensemble = cells.shape[1]
    ones = jnp.full((ensemble, ensemble), 1.0 / ensemble, BF16)
    mean = jnp.dot(cells, ones, preferred_element_type=F32)
    return mean, (cells.astype(F32) - mean).astype(BF16)


def sides(odd, cols):
    last = cols // PATCH - 1
    shift = (1 - 2 * odd).astype(F32) * cols
    return (last * (1 - odd), last * odd), shift


def centre_of(index):
    return jnp.asarray(2 * PATCH * index + PATCH, F32)


def patch_at(r, c):
    return pl.ds(r * PATCH, PATCH), pl.ds(pl.multiple_of(c * PATCH, PATCH), PATCH)


def centres_of(columns):
    return [(centre_of(r), centre_of(c)) for r in range(2) for c in columns]


def eight(ref):
    return [ref.at[4 * edge + 2 * r + at] for r in range(2) for edge in range(2) for at in range(2)]


def own_kernel(odd_ref, own_ref, state_ref, part_ref, mean_ref, perturbation_ref):
    rows, cols, ensemble = state_ref.shape
    edge_columns, _ = sides(odd_ref[0], cols)
    ensemble = own_ref.shape[0] - EXTRA
    block = own_ref[:, : own_ref.shape[1] // 2]
    part = grams_of([block], [(0.0, 0.0)], centres_of(INNER + edge_columns))
    for p, ref in enumerate(eight(part_ref)):
        ref[...] = part[p * ensemble : (p + 1) * ensemble]
    for r in range(rows // 8):
        at = slice(r * 8, (r + 1) * 8)
        mean, perturbation = centred(state_ref[at].reshape(8 * cols, ensemble))
        mean_ref[at] = mean.reshape(8, cols, ensemble)
        perturbation_ref[at] = perturbation.reshape(8, cols, ensemble)


def analyse(mean_ref, perturbation_ref, at, across, transform):
    ensemble = transform.shape[0]
    cells = perturbation_ref[at, across, :].reshape(PATCH * PATCH, ensemble)
    change = jnp.dot(cells, transform, preferred_element_type=F32)
    return (mean_ref[at, across, :] + change.reshape(PATCH, PATCH, ensemble)).astype(BF16)


def mid_kernel(odd_ref, column_ref, part_ref, gram, half, z, right, *, tile):
    edge_columns, _ = sides(odd_ref[0], tile[1])
    add_column(list(zip(eight(part_ref), eight(gram))), column_ref, 0.0, centres_of(INNER + edge_columns), float(tile[0]), own=False)
    inner = patches_of(gram, half, z, right)
    for p in inner:
        begin(p)
    advance(inner[:2], inner[2:], (False, False))
    for _ in range(EARLY_STEPS):
        advance(inner[:2], inner[2:])


def edge_kernel(
    odd_ref, far_ref, near_ref, gram_ref, half_ref, z_ref, mean_ref, perturbation_ref, out_ref, gram, half, z, right, done, semaphores
):
    rows, cols, ensemble = mean_ref.shape
    edge_columns, shift = sides(odd_ref[0], cols)
    half[:4] = half_ref[...]
    z[:4] = z_ref[...]
    inner = patches_of(gram_ref.at[:4], half.at[:4], z.at[:4], right.at[:4])
    edge = patches_of(gram, half.at[4:], z.at[4:], right.at[4:])
    for p in inner:
        p.right[...] = side_by_side(p.half[...])
    columns = []
    for at, (ref, col_shift) in enumerate(((near_ref, shift), (far_ref, -shift))):
        pairs = [(gram_ref.at[4 + 2 * r + at], gram.at[2 * r + at]) for r in range(2)]
        here = centres_of(edge_columns[at : at + 1])
        columns.append(functools.partial(add_column, pairs, ref, col_shift, here, float(rows)))
    advance(inner[:2], inner[2:], fill=iter(columns))
    traces = [begin(p) for p in edge]

    copies = []

    def put(place, at, transform):
        band, across = patch_at(at // 2, place[at % 2])
        slot = len(copies)
        done[slot] = analyse(mean_ref, perturbation_ref, band, across, transform)
        copies.append(pltpu.make_async_copy(done.at[slot], out_ref.at[band, across, :], semaphores.at[slot]))
        copies[slot].start()

    left = NS_STEPS - 3 - EARLY_STEPS
    pieces = iter(finish(inner, lambda at: system_of(inner[at])[1], functools.partial(put, INNER)))
    for step in range(NS_STEPS - 1):
        with_root = step > 0
        if step < left:
            advance(inner, edge, (True, with_root))
        else:
            advance(edge[:2], edge[2:], (with_root, with_root), pieces)
    for piece in pieces:
        piece()
    for piece in finish(edge, lambda at: traces[at], functools.partial(put, edge_columns)):
        piece()
    for copy in copies:
        copy.wait()


def vmem(count):
    return [pl.BlockSpec(memory_space=pltpu.VMEM)] * count


SMEM = pl.BlockSpec(memory_space=pltpu.SMEM)


def pack(members, values, precision, cells, counts, tile_cols):
    capacity, ensemble = members.shape
    given = [pltpu.with_memory_space_constraint(x, pltpu.HBM) for x in (members, values, precision, cells)]
    return pl.pallas_call(
        functools.partial(pack_kernel, tile_cols=tile_cols),
        out_shape=pltpu.VMEM((ensemble + EXTRA, capacity), BF16),
        in_specs=[SMEM] + [pl.BlockSpec(memory_space=pltpu.HBM)] * len(given),
        out_specs=pl.BlockSpec(memory_space=pltpu.VMEM),
        scratch_shapes=[pltpu.VMEM(x.shape, x.dtype) for x in given] + [pltpu.SemaphoreType.DMA((len(given),))],
        compiler_params=pltpu.CompilerParams(vmem_limit_bytes=4 << 20),
    )(counts, *given)


def stack_kernel(own_ref, north_ref, south_ref, late_ref, out_ref, *, tile_rows):
    rows, capacity = own_ref.shape
    kept = capacity // 2
    ensemble = rows - EXTRA
    tiles = (own_ref[...], north_ref[...] + late_ref[...], south_ref[...])
    for at, tile in enumerate(tiles):
        out_ref[:, at * kept : (at + 1) * kept] = tile[:, :kept]
    full = [
        jnp.max(tile[ensemble:, kept:].astype(F32)[WEIGHT : WEIGHT + 1], axis=1, keepdims=True) > 0.0 for tile in tiles[:2]
    ]

    def chosen(own, north, south):
        return jnp.where(full[0], own, jnp.where(full[1], north, south))

    spreads = [tile[:ensemble, kept:].astype(F32) for tile in tiles]
    scalars = [tile[ensemble:, kept:].astype(F32) for tile in tiles]
    index = lax.broadcasted_iota(jnp.int32, (EXTRA, kept), 0)
    shift = chosen(0.0, -float(tile_rows), float(tile_rows))
    out_ref[:ensemble, 3 * kept :] = chosen(*spreads).astype(BF16)
    out_ref[ensemble:, 3 * kept :] = (chosen(*scalars) + jnp.where(index == ROW, shift, 0.0)).astype(BF16)


def stack(own, north, south, late, tile_rows):
    rows, capacity = own.shape
    return pl.pallas_call(
        functools.partial(stack_kernel, tile_rows=tile_rows),
        out_shape=pltpu.VMEM((rows, BLOCKS * (capacity // 2)), BF16),
        in_specs=vmem(4),
        out_specs=pl.BlockSpec(memory_space=pltpu.VMEM),
        compiler_params=pltpu.CompilerParams(vmem_limit_bytes=4 << 20),
    )(own, north, south, late)


def own_part(odd, own, state):
    rows, cols, ensemble = state.shape
    return pl.pallas_call(
        own_kernel,
        out_shape=(
            pltpu.VMEM((8, ensemble, ensemble + EXTRA), F32),
            pltpu.VMEM(state.shape, F32),
            pltpu.VMEM(state.shape, BF16),
        ),
        in_specs=[SMEM] + vmem(2),
        out_specs=tuple(vmem(3)),
        compiler_params=pltpu.CompilerParams(vmem_limit_bytes=12 << 20),
        cost_estimate=pl.CostEstimate(flops=1 << 30, bytes_accessed=1 << 20, transcendentals=0),
    )(odd, own, state)


def middle(odd, column, part, tile):
    ensemble = part.shape[1]
    return pl.pallas_call(
        functools.partial(mid_kernel, tile=tile),
        out_shape=(
            pltpu.VMEM(part.shape, F32),
            pltpu.VMEM((4, ensemble, ensemble), F32),
            pltpu.VMEM((4, ensemble, ensemble), F32),
        ),
        in_specs=[SMEM] + vmem(2),
        out_specs=tuple(vmem(3)),
        scratch_shapes=[pltpu.VMEM((4, ensemble, 2 * ensemble), BF16)],
        compiler_params=pltpu.CompilerParams(vmem_limit_bytes=12 << 20),
        cost_estimate=pl.CostEstimate(flops=1 << 32, bytes_accessed=1 << 20, transcendentals=0),
    )(odd, column, part)


def edges(odd, near, far, gram, half, z, mean, perturbation):
    ensemble = mean.shape[-1]
    return pl.pallas_call(
        edge_kernel,
        out_shape=jax.ShapeDtypeStruct(mean.shape, BF16),
        in_specs=[SMEM] + vmem(7),
        out_specs=pl.BlockSpec(memory_space=pltpu.HBM),
        scratch_shapes=[
            pltpu.VMEM((4, *gram.shape[1:]), F32),
            pltpu.VMEM((8, ensemble, ensemble), F32),
            pltpu.VMEM((8, ensemble, ensemble), F32),
            pltpu.VMEM((8, ensemble, 2 * ensemble), BF16),
            pltpu.VMEM((8, PATCH, PATCH, ensemble), BF16),
            pltpu.SemaphoreType.DMA((8,)),
        ],
        compiler_params=pltpu.CompilerParams(vmem_limit_bytes=12 << 20),
    )(odd, far, near, gram, half, z, mean, perturbation)


def shifts(x):
    count = lax.axis_size("lat")
    upper = count // 2 - 1
    southward = [(i, i + 1) for i in range(count - 1) if i + 1 != upper]
    northward = [(i + 1, i) for i in range(count - 1)]
    return [lax.ppermute(x, "lat", pairs) for pairs in (southward, northward, [(upper - 1, upper)])]


def exchange(x, axis, first):
    count = lax.axis_size(axis)
    pairs = []
    for low in range(first, count, 2):
        high = (low + 1) % count
        pairs += [(low, high), (high, low)]
    return lax.ppermute(x, axis, pairs)


def body(state, obs_members, obs_values, obs_precision, obs_cells, obs_counts):
    _, tile_rows, tile_cols, ensemble = state.shape
    capacity = obs_members.shape[2]
    odd = (lax.axis_index("lon") & 1).astype(jnp.int32).reshape(1)
    own = pack(
        obs_members.reshape(capacity, ensemble),
        obs_values.reshape(1, capacity),
        obs_precision.reshape(1, capacity),
        obs_cells.reshape(1, capacity),
        obs_counts,
        tile_cols,
    )
    column = stack(own, *shifts(own), tile_rows)
    far = exchange(column, "lon", 1)
    near = exchange(column, "lon", 0)
    part, mean, perturbation = own_part(odd, own, state.reshape(tile_rows, tile_cols, ensemble))
    gram, half, z = middle(odd, column, part, (tile_rows, tile_cols))
    out = edges(odd, near, far, gram, half, z, mean, perturbation)
    return out.reshape(state.shape)


def solution(mesh):
    in_specs = (
        P(None, "lat", "lon", None),
        P("lat", "lon", None, None),
        P("lat", "lon", None),
        P("lat", "lon", None),
        P("lat", "lon", None),
        P("lat", "lon"),
    )
    out_specs = P(None, "lat", "lon", None)
    return jax.shard_map(body, mesh=mesh, in_specs=in_specs, out_specs=out_specs, check_vma=False)
```
